32 devices in a mesh: dp: 8 (over y, x, core), mp: 4 (over z).
Axes of the slice: x: 2, y: 2, z: 4, core: 2. Of those that a mesh axis runs over, the one named last changes fastest.
Arguments:
- tokens: bfloat16 [8192, 768], P('dp', 'mp'), may hold values from -6 to 6
- cotangent: bfloat16 [8192, 768], P('dp', 'mp'), may hold values from -6 to 6
- seg_ids: int32 [8, 1024], P('dp'), may hold values from 0 to 3, never falling along the last dimension, each value on 1 to 512 neighbouring positions
- row_lengths: int32 [8], P('dp'), may hold values from 512 to 1024
- group_tags: int32 [8, 4], P('dp'), may hold values from 0 to 3
- group_weights: int32 [4], replicated, may hold values from 1 to 4
- gain_one: float32 [768], P('mp'), may hold values from 0.5 to 1.5
- shift_one: float32 [768], P('mp'), may hold values from -1.75 to 1.75
- w_in: bfloat16 [3, 768, 768], P(None, None, 'mp'), may hold values from -0.21875 to 0.21875
- b_in: float32 [3, 768], P(None, 'mp'), may hold values from -1.75 to 1.75
- taps: float32 [3, 3, 768], P(None, None, 'mp'), may hold values from -3.5 to 3.5
- f_one: float32 [33, 64], replicated, may hold values from -1 to 1
- c_one: float32 [64], replicated, may hold values from -6 to 6
- f_two: float32 [64, 64], replicated, may hold values from -0.75 to 0.75
- c_two: float32 [64], replicated, may hold values from -6 to 6
- sine_freq: float32 [2, 64], replicated, may hold values from 0.6 to 1.4
- f_three: float32 [64, 768], P(None, 'mp'), may hold values from -0.0234375 to 0.0234375
- c_three: float32 [768], P('mp'), may hold values from -0.1875 to 0.1875
- decay: float32 [768], P('mp'), may hold values from 0.5 to 40
- conv_bias: float32 [768], P('mp'), may hold values from -6 to 6
- w_out: bfloat16 [768, 768], P('mp'), may hold values from -0.21875 to 0.21875
- b_out: float32 [768], P('mp'), may hold values from -1.75 to 1.75
- gain_two: float32 [768], P('mp'), may hold values from 0.5 to 1.5
- shift_two: float32 [768], P('mp'), may hold values from -1.75 to 1.75
- w_up: bfloat16 [768, 3072], P(None, 'mp'), may hold values from -0.21875 to 0.21875
- b_up: float32 [3072], P('mp'), may hold values from -1.75 to 1.75
- w_down: bfloat16 [3072, 768], P('mp'), may hold values from -0.109375 to 0.109375
- b_down: float32 [768], P('mp'), may hold values from -1.75 to 1.75
Outputs:
- output: float32 [8192, 768], P('dp', 'mp')
- d_tokens: float32 [8192, 768], P('dp', 'mp')
- d_gain_one: float32 [768], P('mp')
- d_shift_one: float32 [768], P('mp')
- d_w_in: float32 [3, 768, 768], P(None, None, 'mp')
- d_b_in: float32 [3, 768], P(None, 'mp')
- d_taps: float32 [3, 3, 768], P(None, None, 'mp')
- d_f_one: float32 [33, 64], replicated
- d_c_one: float32 [64], replicated
- d_f_two: float32 [64, 64], replicated
- d_c_two: float32 [64], replicated
- d_sine_freq: float32 [2, 64], replicated
- d_f_three: float32 [64, 768], P(None, 'mp')
- d_c_three: float32 [768], P('mp')
- d_decay: float32 [768], P('mp')
- d_conv_bias: float32 [768], P('mp')
- d_w_out: float32 [768, 768], P('mp')
- d_b_out: float32 [768], P('mp')
- d_gain_two: float32 [768], P('mp')
- d_shift_two: float32 [768], P('mp')
- d_w_up: float32 [768, 3072], P(None, 'mp')
- d_b_up: float32 [3072], P('mp')
- d_w_down: float32 [3072, 768], P('mp')
- d_b_down: float32 [768], P('mp')
- penalty: float32 [], replicated
The draws below stay inside these ranges and needn't reach their ends.
All inputs are finite; a program needn't handle non-finite values.
Results may differ from the reference program's by a relative error of at most 0.0074.
Values may be sent and summed in bfloat16 or wider, within the bound.
A program may use at most 128 MiB of HBM per device.

```python
import math
import jax
import jax.numpy as jnp
import numpy as np
from jax import lax

D = 768
FF = 3072
FILT = 64
EMB = 33
LEN = 1024
SEGS = 4
GROUPS = 4
ROWS = 8
TOKENS = 8192


def touch_ends(drawn, rng, least, top_value):
    dims = drawn.shape
    index_at = [jax.random.randint(jax.random.fold_in(rng, axis), (), 0, dims[axis]) for axis in range(len(dims))]
    drawn = drawn.at[tuple(index_at)].set(least)
    longest = dims.index(max(dims))
    index_at[longest] = (index_at[longest] + 1) % dims[longest]
    return drawn.at[tuple(index_at)].set(top_value)


def steps_of(rng, shape, pieces, low, largest):
    def one(dim, shards_of):
        steps = jax.random.uniform(jax.random.fold_in(jax.random.fold_in(rng, 6), dim), (shards_of,), jnp.float32, low / len(pieces), largest / len(pieces))
        return jnp.repeat(jnp.exp(steps), shape[dim] // shards_of).reshape((-1,) + (1,) * (len(shape) - dim - 1))

    factor_of = one(*pieces[0])
    for cut in pieces[1:]:
        factor_of = factor_of * one(*cut)
    return factor_of


def length_profile(count, total, limit, lean):
    portions = [(1 << 20) // math.isqrt(rank ** lean) + 1 for rank in range(2, count + 1)]
    surplus, counts = total - limit - (count - 1), [1] * (count - 1)
    while surplus > 0:
        movable = [i for i in range(count - 1) if counts[i] < limit]
        pool, remaining = sum([portions[i] for i in movable]), surplus
        for i in movable:
            more = min(limit - counts[i], max(1, remaining * portions[i] // pool), surplus)
            counts[i] = counts[i] + more
            surplus = surplus - more
    return np.array([limit] + counts)


def uneven(rng, number_of, total, bound, skew):
    if number_of == 2:
        one = jax.random.randint(rng, (), max(1, total - bound), min(bound, total - 1) + 1)
        return jnp.stack([one, total - one])
    sizes = jnp.asarray(length_profile(number_of, total, bound, skew), jnp.int32)
    couples = (number_of - 1) // 2
    giver, taker = sizes[1:1 + 2 * couples:2], sizes[2:2 + 2 * couples:2]
    margin = jnp.minimum(giver - 1, bound - taker)
    passed = jax.random.randint(jax.random.fold_in(rng, 1), (couples,), 0, 1 << 20) % (margin + 1)
    sizes = sizes.at[1:1 + 2 * couples:2].set(giver - passed).at[2:2 + 2 * couples:2].set(taker + passed)
    return sizes[jax.random.permutation(jax.random.fold_in(rng, 2), number_of)]


def centred(rng, dims, width, reach, shards=(), kind=jnp.bfloat16):
    array = jax.random.normal(rng, dims, jnp.float32) * width
    if len(shards) > 0:
        array = steps_of(rng, dims, shards, -0.22, 0.18) * array
    return jnp.clip(array, min=-reach, max=reach).astype(kind)


def setup_inputs(seed: int = 0) -> dict:
    keys = jax.random.split(jax.random.key(seed), 29)
    tokens = centred(keys[0], (TOKENS, D), 1.0, 6.0, ((0, 8), (1, 4)))
    cotangent = centred(keys[1], (TOKENS, D), 1.0, 6.0, ((0, 8), (1, 4)))
    seg_ids = jax.vmap(lambda own: jnp.searchsorted(jnp.cumsum(uneven(own, SEGS, LEN, LEN // 2, 0)), jnp.arange(LEN), side="right"))(jax.random.split(keys[2], ROWS)).reshape((ROWS, LEN)).astype(jnp.int32)
    row_lengths = touch_ends(jax.random.randint(keys[3], (ROWS,), LEN // 2, LEN + 1), jax.random.fold_in(keys[3], 1), LEN // 2, LEN).astype(jnp.int32)
    group_tags = touch_ends(jax.random.randint(keys[4], (ROWS, SEGS), 0, GROUPS), jax.random.fold_in(keys[4], 1), 0, GROUPS - 1).astype(jnp.int32)
    group_weights = touch_ends(jax.random.randint(keys[5], (GROUPS,), 1, 5), jax.random.fold_in(keys[5], 1), 1, 4).astype(jnp.int32)
    gain_one = jnp.clip(1.0 + 0.1 * jax.random.normal(keys[6], (D,), jnp.float32), 0.5, 1.5)
    shift_one = centred(keys[7], (D,), 0.3, 1.75, ((0, 4),), jnp.float32)
    w_in = centred(keys[8], (3, D, D), D ** -0.5, 0.21875, ((2, 4),))
    b_in = centred(keys[9], (3, D), 0.3, 1.75, ((1, 4),), jnp.float32)
    taps = centred(keys[10], (3, 3, D), 0.6, 3.5, ((2, 4),), jnp.float32)
    f_one = centred(keys[11], (EMB, FILT), EMB ** -0.5, 1.0, (), jnp.float32)
    c_one = centred(keys[12], (FILT,), 1.0, 6.0, (), jnp.float32)
    f_two = centred(keys[13], (FILT, FILT), FILT ** -0.5, 0.75, (), jnp.float32)
    c_two = centred(keys[14], (FILT,), 1.0, 6.0, (), jnp.float32)
    sine_freq = jnp.clip(jax.random.uniform(keys[15], (2, FILT), jnp.float32, 0.6, 1.4), 0.6, 1.4)
    f_three = centred(keys[16], (FILT, D), (FILT * LEN) ** -0.5, 0.0234375, ((1, 4),), jnp.float32)
    c_three = centred(keys[17], (D,), (LEN ** -0.5), 0.1875, ((0, 4),), jnp.float32)
    decay = jnp.clip(jnp.exp(math.log(40.0) - 4.3820266 * jax.random.uniform(keys[18], (D,), jnp.float32) ** steps_of(keys[18], (D,), ((0, 4),), -0.2, 0.2)), 0.5, 40.0)
    conv_bias = centred(keys[19], (D,), 1.0, 6.0, ((0, 4),), jnp.float32)
    w_out = centred(keys[20], (D, D), D ** -0.5, 0.21875, ((0, 4),))
    b_out = centred(keys[21], (D,), 0.3, 1.75, ((0, 4),), jnp.float32)
    gain_two = jnp.clip(1.0 + 0.1 * jax.random.normal(keys[22], (D,), jnp.float32), 0.5, 1.5)
    shift_two = centred(keys[23], (D,), 0.3, 1.75, ((0, 4),), jnp.float32)
    w_up = centred(keys[24], (D, FF), D ** -0.5, 0.21875, ((1, 4),))
    b_up = centred(keys[25], (FF,), 0.3, 1.75, ((0, 4),), jnp.float32)
    w_down = centred(keys[26], (FF, D), FF ** -0.5, 0.109375, ((0, 4),))
    b_down = centred(keys[27], (D,), 0.3, 1.75, ((0, 4),), jnp.float32)
    return {"tokens": tokens, "cotangent": cotangent, "seg_ids": seg_ids, "row_lengths": row_lengths, "group_tags": group_tags, "group_weights": group_weights, "gain_one": gain_one, "shift_one": shift_one, "w_in": w_in, "b_in": b_in, "taps": taps, "f_one": f_one, "c_one": c_one, "f_two": f_two, "c_two": c_two, "sine_freq": sine_freq, "f_three": f_three, "c_three": c_three, "decay": decay, "conv_bias": conv_bias, "w_out": w_out, "b_out": b_out, "gain_two": gain_two, "shift_two": shift_two, "w_up": w_up, "b_up": b_up, "w_down": w_down, "b_down": b_down}


@jax.custom_vjp
def low(v):
    return lax.optimization_barrier(v.astype(jnp.bfloat16)).astype(jnp.float32)

@jax.custom_vjp
def low_back(v):
    return v

def low_keep(v):
    return (low(v), None)

def low_pass(kept, grad):
    return (grad,)

def back_keep(v):
    return (v, None)

def back_low(kept, grad):
    return (low(grad),)
low.defvjp(low_keep, low_pass)
low_back.defvjp(back_keep, back_low)
epsilon = 1e-05
pen_coef = 0.5
highest = lax.Precision.HIGHEST

def positions():
    places = jnp.arange(LEN, dtype=jnp.int32)
    band_index = jnp.arange(1, (EMB - 1) // 2 + 1, dtype=jnp.int32)
    phase_turn = places[:, None] * band_index[None, :] % LEN
    angles = phase_turn.astype(jnp.float32) * (2.0 * jnp.pi / LEN)
    position_ramp = places.astype(jnp.float32)[:, None] / LEN
    return jnp.concatenate([position_ramp, jnp.cos(angles), jnp.sin(angles)], axis=1)

def make_filter(f_one, c_one, f_two, c_two, sine_freq, f_three, c_three, decay):
    embedded = positions()
    hidden_one = jnp.sin(sine_freq[0] * (jnp.dot(embedded, f_one, precision=highest) + c_one))
    hidden_two = jnp.sin(sine_freq[1] * (jnp.dot(hidden_one, f_two, precision=highest) + c_two))
    raw_kernel = jnp.dot(hidden_two, f_three, precision=highest) + c_three
    time_ramp = jnp.arange(LEN, dtype=jnp.int32).astype(jnp.float32)[:, None] / LEN
    kernel = raw_kernel * jnp.exp(-decay[None, :] * time_ramp)
    tail_energy = lax.optimization_barrier(jnp.mean(kernel[LEN // 2:] ** 2, axis=0))
    whole_energy = lax.optimization_barrier(jnp.mean(kernel ** 2, axis=0)) + 1e-06
    return (kernel, jnp.sum(tail_energy / whole_energy))

def layer_norm(row_values, gain, shift):
    centre = lax.optimization_barrier(jnp.mean(row_values, axis=-1, keepdims=True))
    spread = lax.optimization_barrier(jnp.mean((row_values - centre) ** 2, axis=-1, keepdims=True))
    return (row_values - centre) * lax.rsqrt(spread + epsilon) * gain + shift

def short_conv(fields, taps):
    padded = jnp.pad(fields, ((0, 0), (2, 0), (0, 0)))
    return taps[:, 0, None, :] * fields + taps[:, 1, None, :] * padded[:, 1:LEN + 1] + taps[:, 2, None, :] * padded[:, 0:LEN]

def causal_conv(signal, kernel):
    full_size = 2 * LEN
    product = jnp.fft.rfft(signal, n=full_size, axis=0) * jnp.fft.rfft(kernel, n=full_size, axis=0)
    return jnp.fft.irfft(product, n=full_size, axis=0)[:LEN]

def row_block(one_row, kernel, gain_one, shift_one, w_in, b_in, taps, conv_bias, w_out, b_out, gain_two, shift_two, w_up, b_up, w_down, b_down):
    normed = low(layer_norm(one_row, gain_one, shift_one))
    fields = low_back(jnp.einsum('td,jdc->jtc', normed, w_in, precision=highest)) + b_in[:, None, :]
    short_out = short_conv(fields, taps)
    gated = short_out[2] * short_out[1]
    long_out = causal_conv(gated, kernel) + conv_bias * gated
    outer = low(long_out * short_out[0])
    residual = one_row + low_back(jnp.dot(outer, w_out, precision=highest)) + b_out
    normed_two = low(layer_norm(residual, gain_two, shift_two))
    hidden = low_back(jnp.dot(normed_two, w_up, precision=highest)) + b_up
    active = low(jax.nn.gelu(hidden, approximate=False))
    return residual + low_back(jnp.dot(active, w_down, precision=highest)) + b_down

def token_weights(seg_ids, row_lengths, group_tags, group_weights):
    seg_pick = (seg_ids[:, :, None] == jnp.arange(SEGS, dtype=jnp.int32)[None, None, :]).astype(jnp.int32)
    row_tag = lax.optimization_barrier(jnp.sum(seg_pick * group_tags[:, None, :], axis=2))
    group_pick = (row_tag[:, :, None] == jnp.arange(GROUPS, dtype=jnp.int32)[None, None, :]).astype(jnp.int32)
    weight_int = lax.optimization_barrier(jnp.sum(group_pick * group_weights[None, None, :], axis=2))
    places = jnp.arange(LEN, dtype=jnp.int32)[None, :]
    live_mask = (places < row_lengths[:, None]).astype(jnp.int32)
    return (weight_int * live_mask).astype(jnp.float32)

def reference(tokens, cotangent, seg_ids, row_lengths, group_tags, group_weights, gain_one, shift_one, w_in, b_in, taps, f_one, c_one, f_two, c_two, sine_freq, f_three, c_three, decay, conv_bias, w_out, b_out, gain_two, shift_two, w_up, b_up, w_down, b_down):
    (kernel, pen_total), filter_pull = jax.vjp(make_filter, f_one, c_one, f_two, c_two, sine_freq, f_three, c_three, decay)
    layer_args = (gain_one, shift_one, w_in.astype(jnp.float32), b_in, taps, conv_bias, w_out.astype(jnp.float32), b_out, gain_two, shift_two, w_up.astype(jnp.float32), b_up, w_down.astype(jnp.float32), b_down)
    token_rows = tokens.astype(jnp.float32).reshape(ROWS, LEN, D)
    weighting = token_weights(seg_ids, row_lengths, group_tags, group_weights)
    scaled = cotangent.astype(jnp.float32).reshape(ROWS, LEN, D) * weighting[:, :, None]

    def row_step(totals, pair_item):
        one_row, one_cot = pair_item
        result, row_pull = jax.vjp(row_block, one_row, kernel, *layer_args)
        row_grads = row_pull(one_cot)
        return (jax.tree.map(jnp.add, totals, tuple(row_grads[1:])), (result, row_grads[0]))
    zero_sums = jax.tree.map(jnp.zeros_like, (kernel,) + layer_args)
    totals, (results, d_rows) = lax.scan(row_step, zero_sums, (token_rows, scaled))
    filter_grads = filter_pull((totals[0], jnp.asarray(pen_coef / D, jnp.float32)))
    layer_grads = totals[1:]
    return (results.reshape(TOKENS, D), d_rows.reshape(TOKENS, D), layer_grads[0], layer_grads[1], layer_grads[2], layer_grads[3], layer_grads[4], filter_grads[0], filter_grads[1], filter_grads[2], filter_grads[3], filter_grads[4], filter_grads[5], filter_grads[6], filter_grads[7], layer_grads[5], layer_grads[6], layer_grads[7], layer_grads[8], layer_grads[9], layer_grads[10], layer_grads[11], layer_grads[12], layer_grads[13], pen_total / D)
```

```python
import functools
import math

import jax
import jax.numpy as jnp
import ml_dtypes
import numpy as np
from jax import lax
from jax.experimental import pallas as pl
from jax.experimental.pallas import tpu as pltpu
from jax.sharding import PartitionSpec as P

EMB = 33
SEGS = 4
GROUPS = 4
FILT = 64
MP = 4
epsilon = 1e-05
pen_coef = 0.5
HI = lax.Precision.HIGHEST
MESH = pl.DeviceIdType.MESH
bf = jnp.bfloat16
f32 = jnp.float32
NSEM = 200


def dg(left, right, left_dim, right_dim, **kw):
    return lax.dot_general(
        left, right, (((left_dim,), (right_dim,)), ((), ())), preferred_element_type=f32, **kw
    )


def tables(seq):
    t = np.arange(seq)
    ang = (np.outer(t, t) % (2 * seq)) * (2.0 * np.pi / (2 * seq))
    cos, sin = np.cos(ang), np.sin(ang)
    fwd = np.concatenate([cos, -sin], axis=1)
    alt = np.where(t % 2 == 0, 1.0, -1.0)
    fwd[:, seq] = alt
    emb = np.zeros((128, seq))
    emb[0] = t / seq
    for m in range(1, (EMB - 1) // 2 + 1):
        a = (t * m % seq) * (2.0 * np.pi / seq)
        emb[m] = np.cos(a)
        emb[(EMB - 1) // 2 + m] = np.sin(a)
    low = lambda v: v.astype(np.float32).astype(ml_dtypes.bfloat16)
    return low(fwd), emb.astype(np.float32)


def main_kernel(
    nbits, dp_size, dims,
    tok_h, cot_h, win_h, wout_h, wup_h, wdn_h, F_h, emb_h,
    seg_r, len_r, tag_r, gw_r, g1_r, s1_r, bin_r, taps_r, f1_r, c1_r, f2_r, c2_r, sq_r, f3_r, c3_r,
    dec_r, cb_r, bo_r, g2_r, s2_r, bu_r, bd_r,
    outb_o, dtok_o, gup_o, gdn_o, gwo_o, gin_o, sm1_o, sm2_o, sm3_o, sm4_o,
    tokF, cotB, cotK, n1F, winv, F, emb, zf, sf, yv, pv, kv, KS, PS, XS,
    oB, oK, WO, WU, WD, rv, xh2, n2P, goP, gv, dav, wt, stat, PG, COLS,
    brS, brR, dnS, dnR, outB, drB, doS, doB, dnO, brO,
    GU, RU0, RU1, RUz, GD, RD0, RD1, RDz, GO, RO0, RO1, RO2, RO3, FO,
    GI, RI0, RI1, RI2, FI, dzf, stS, stR, SAc, SM1, SM1r, SM3, SM3r, SM2, SM2r, SMz3, SMz2,
    SM4, SM4r, XGI, h1s, h2s, u1s, u2s, dks, dsv, prow, pcol_r, bup, fz, frow,
    gfree, credit, ssem, rsem, lsem, ss_tok, rs_tok, ss_rs, rs_rs, ss_sp, rs_sp,
):
    T, C, D = dims
    TB = T // MP
    d = lax.axis_index("dp")
    m = lax.axis_index("mp")
    bits = [(d // 2**b) % 2 for b in range(nbits)]
    dnb = [(d + (1 - 2 * bits[b]) * 2**b, m) for b in range(nbits)]
    peer = {1: m + 1 - 2 * (m % 2), 2: (m + 2) % 4, 3: 3 - m}
    pdev = {k: (d, peer[k]) for k in peer}
    slot = [m, peer[1], peer[2], peer[3]]
    used = [0]
    pending = []

    def rc(src, dst, dev):
        i = used[0]
        used[0] += 1
        c = pltpu.make_async_remote_copy(
            src_ref=src, dst_ref=dst, send_sem=ssem.at[i], recv_sem=rsem.at[i],
            device_id=dev, device_id_type=MESH,
        )
        c.start()
        pending.append(c)
        return c

    lused = [0]

    def lc(src, dst):
        i = lused[0]
        lused[0] += 1
        c = pltpu.make_async_copy(src, dst, lsem.at[i])
        c.start()
        return c

    def recv(cs):
        for c in cs:
            c.wait_recv()

    FU, FD = WU, WD
    H = D // 2
    QU, QD = D // 4, D // 8
    x0, x1, x2 = bits[0], bits[1], bits[2]
    xU, xD = (x1, x2), (x2, x1)
    pU, pD = 2 * x1 + x2, 2 * x2 + x1
    outS, drS = oB, cotB

    def sent(cs):
        for c in cs:
            c.wait_send()
            pending[:] = [p for p in pending if p is not c]

    c_tok = [lc(tok_h.at[:, pl.ds(TB * b, TB)], tokF.at[m, b]) for b in range(MP)]
    c_cot = [lc(cot_h.at[:, pl.ds(TB * b, TB)], cotB.at[b]) for b in range(MP)]
    c_wo = [lc(wout_h.at[:, pl.ds(h * (D // 2), D // 2)], WO.at[h, m]) for h in range(2)]
    c_win = lc(win_h, winv)
    c_emb = lc(emb_h, emb)
    c_F = lc(F_h, F)
    half = pl.ds(pl.multiple_of(H * x0, H), H)
    c_own = []
    for p in range(4):
        c_own.append(lc(wup_h.at[pl.ds(QU * p, QU), half], WU.at[m, p // 2, p % 2]))
        c_own.append(lc(wdn_h.at[pl.ds(pl.multiple_of(H * x0 + QD * p, QD), QD)], WD.at[m, p // 2, p % 2]))

    barrier = pltpu.get_barrier_semaphore()
    for dev in list(pdev.values()) + dnb:
        pl.semaphore_signal(barrier, inc=1, device_id=dev, device_id_type=MESH)
    pl.semaphore_wait(barrier, 3 + nbits)

    right = (d, lax.rem(m + 1, MP))
    left = (d, lax.rem(m + MP - 1, MP))
    NC = MP + 2

    def relay(way, step, chunk, shard, dev):
        i = (way * 3 + step) * NC + chunk
        if chunk == 4:
            ref = WU.at[shard, xU[0], xU[1]]
        elif chunk == 5:
            ref = WD.at[shard, xD[0], xD[1]]
        else:
            ref = tokF.at[shard, chunk]
        return pltpu.make_async_remote_copy(
            src_ref=ref, dst_ref=ref, send_sem=ss_tok.at[i], recv_sem=rs_tok.at[i],
            device_id=dev, device_id_type=MESH,
        )

    def relay_own(chunk):
        @pl.when(m < MP - 1)
        def _():
            relay(0, 0, chunk, m, right).start()

        @pl.when(m > 0)
        def _():
            relay(1, 0, chunk, m, left).start()

    def relay_on(step, chunk):
        @pl.when(m - 1 - step >= 0)
        def _():
            relay(0, step, chunk, m - 1 - step, right).wait_recv()

        @pl.when(m + 1 + step < MP)
        def _():
            relay(1, step, chunk, m + 1 + step, left).wait_recv()

        if step < 2:
            @pl.when(jnp.logical_and(m - 1 - step >= 0, m < MP - 1))
            def _():
                relay(0, step + 1, chunk, m - 1 - step, right).start()

            @pl.when(jnp.logical_and(m + 1 + step < MP, m > 0))
            def _():
                relay(1, step + 1, chunk, m + 1 + step, left).start()

    for b in range(MP):
        c_tok[b].wait()
        relay_own(b)

    for i, ref in enumerate((g1_r, s1_r, g2_r, s2_r, bo_r, bd_r)):
        PG[m, i : i + 1, :] = ref[...].reshape(1, C)
    brow = bu_r[...].reshape(1, D)
    bup[m] = jnp.zeros((8, H), f32)
    bup[m, 0:1, :] = jnp.where(x0 == 0, brow[:, 0:H], brow[:, H:D])
    c_pg = [rc(PG.at[m], PG.at[m], pdev[k]) for k in (1, 2, 3)]
    c_pg += [rc(bup.at[m], bup.at[m], pdev[k]) for k in (1, 2, 3)]

    for c in c_wo:
        c.wait()
    WR = C // 4
    ordO = (0, 1, 2)

    def wo_send(rows, dev):
        return [rc(WO.at[x0, peer[k], rows], WO.at[x0, peer[k], rows], dev) for k in (1, 2, 3)]

    WR1 = pl.ds(WR * (2 * x1 + x2), WR)
    c_wop = [rc(WO.at[x0, m, WR1], WO.at[x0, m, WR1], pdev[k]) for k in (1, 2, 3)]

    def spread(way, step, stage, wait=False):
        shard = m - 1 - step if way == 0 else m + 1 + step

        @pl.when(shard >= 0 if way == 0 else shard < MP)
        def _():
            for e, (W, x, nb) in enumerate(((WU, xU, (dnb[2], dnb[1])), (WD, xD, (dnb[1], dnb[2])))):
                ref = W.at[shard, x[0], x[1]] if stage == 0 else W.at[shard, x[0]]
                i = ((way * 3 + step) * 2 + stage) * 2 + e
                c = pltpu.make_async_remote_copy(
                    src_ref=ref, dst_ref=ref, send_sem=ss_sp.at[i], recv_sem=rs_sp.at[i],
                    device_id=nb[stage], device_id_type=MESH,
                )
                if wait == "send":
                    c.wait_send()
                elif wait:
                    c.wait_recv()
                else:
                    c.start()

    def spread_step(step, stage, wait=False):
        for way in range(2):
            spread(way, step, stage, wait)

    seg = seg_r[...]
    tag = jnp.zeros((1, T), jnp.int32)
    for s in range(SEGS):
        tag = jnp.where(seg == s, tag_r[0, s], tag)
    wi = jnp.zeros((1, T), jnp.int32)
    for g in range(GROUPS):
        wi = jnp.where(tag == g, gw_r[g], wi)
    place = lax.broadcasted_iota(jnp.int32, (1, T), 1)
    wi = jnp.where(place < len_r[0], wi, 0)
    wf = wi.astype(f32)
    for b in range(MP):
        wt[b, 0:1, :] = wf[:, TB * b : TB * b + TB]

    relay_on(0, 0)

    prow[...] = jnp.zeros_like(prow)
    for i, ref in ((0, g1_r), (1, s1_r), (14, c3_r), (15, dec_r), (16, cb_r)):
        prow[i : i + 1, :] = ref[...].reshape(1, C)
    prow[2:5, :] = bin_r[...]
    for j in range(3):
        prow[5 + 3 * j : 8 + 3 * j, :] = taps_r[j]
    pcol_r[...] = prow[...].T

    SAc[...] = jnp.zeros_like(SAc)
    dbd = jnp.zeros((C, 1), f32)
    for b in range(MP):
        c_cot[b].wait()
        dbd = dbd + jnp.sum(cotB[b].astype(f32) * wf[:, TB * b : TB * b + TB], axis=1, keepdims=True)
    SAc[:, 17:18] = dbd
    COLS[...] = jnp.zeros_like(COLS)

    relay_on(0, 1)

    ROWS = 48

    def chunks(n, fn, step=ROWS):
        @pl.loop(0, n // step)
        def _(i):
            fn(pl.ds(pl.multiple_of(i * step, step), step))

    NB = 512

    def spectrum(parts, out):
        for n in range(0, 2 * T, NB):
            acc = dg(parts[0][...], F[:, n : n + NB], 1, 0)
            for part in parts[1:]:
                acc = acc + dg(part[...], F[:, n : n + NB], 1, 0)
            out[:, n : n + NB] = acc

    def inverse(out, low=None):
        for n in range(0, T, NB // 2):
            rows = slice(n, n + NB // 2)
            acc = dg(XS[...], F[rows, :], 1, 1)
            if low is not None:
                for e in range(2):
                    acc = acc + dg(low[e * C : (e + 1) * C], F[rows, e * T : e * T + T], 1, 1)
            out[:, rows] = acc

    def two(x):
        hi = x.astype(bf)
        return hi, (x - hi.astype(f32)).astype(bf)

    tramp = place.astype(f32) * (1.0 / T)
    fz[...] = jnp.zeros_like(fz)
    fz[0:EMB, :] = f1_r[...]
    frow[...] = jnp.zeros_like(frow)
    frow[0:1, :] = c1_r[...].reshape(1, FILT)
    frow[1:2, :] = c2_r[...].reshape(1, FILT)
    frow[2:4, :] = sq_r[...]
    fcol = frow[...].T
    c1, c2, q0, q1s = (fcol[:, i : i + 1] for i in range(4))
    c_emb.wait()
    w1 = dg(fz[...], emb[...], 0, 0, precision=HI) + c1
    u1s[...] = w1
    h1 = jnp.sin(q0 * w1)
    h1s[...] = h1
    w2 = dg(f2_r[...], h1, 0, 0, precision=HI) + c2
    u2s[...] = w2
    h2 = jnp.sin(q1s * w2)
    h2s[...] = h2
    relay_on(0, 2)
    kv[...] = dg(f3_r[...], h2, 0, 0, precision=HI)

    def kern_rows(r):
        k = (kv[r] + pcol_r[r, 14:15]) * jnp.exp(-pcol_r[r, 15:16] * tramp)
        kv[r] = k
        XS[r, 0:T], XS[r, T : 2 * T] = two(k)

    chunks(C, kern_rows)
    relay_on(0, 3)
    c_F.wait()
    XSh = [XS.at[:, pl.ds(0, T)], XS.at[:, pl.ds(T, T)]]
    spectrum(XSh, KS)

    recv(c_wop)
    c_wo2 = wo_send(WR1, dnb[2])
    for b in range(MP):
        relay_on(1, b)
    for c in c_own:
        c.wait()
    relay_own(4)
    relay_own(5)
    recv(c_wo2)
    c_wo2 = wo_send(pl.ds(2 * WR * x1, 2 * WR), dnb[1])

    recv(c_pg)
    for s in range(MP):
        COLS[s * C : (s + 1) * C, 0:8] = PG[s].T
    for k in range(MP):
        COLS[0:H, 64 + 8 * k : 72 + 8 * k] = bup[slot[k]].T

    c_win.wait()

    def norm_block(b):
        tot = jnp.zeros((1, TB), f32)
        for s in range(MP):
            tot = tot + jnp.sum(tokF[s, b].astype(f32), axis=0, keepdims=True)
        mu = tot * (1.0 / D)
        tot = jnp.zeros((1, TB), f32)
        for s in range(MP):
            xc = tokF[s, b].astype(f32) - mu
            tot = tot + jnp.sum(xc * xc, axis=0, keepdims=True)
        sc = lax.rsqrt(tot * (1.0 / D) + epsilon)
        for s in range(MP):
            r = slice(s * C, s * C + C)
            xh = (tokF[s, b].astype(f32) - mu) * sc
            n1F[r, TB * b : TB * b + TB] = (xh * COLS[r, 0:1] + COLS[r, 1:2]).astype(bf)
        n1 = n1F[:, TB * b : TB * b + TB]
        stat[0:1, TB * b : TB * b + TB] = mu
        stat[1:2, TB * b : TB * b + TB] = sc
        for j in range(3):
            zf[j, :, TB * b : TB * b + TB] = dg(winv[j], n1, 1, 0) + pcol_r[:, 2 + j : 3 + j]

    for b in range(MP):
        relay_on(2, b)
        norm_block(b)
    recv(c_wo2)
    c_wo2 = wo_send(pl.ds(0, C), dnb[0])
    relay_on(0, 4)
    relay_on(0, 5)
    spread_step(0, 0)

    lane = lax.broadcasted_iota(jnp.int32, (1, T), 1)
    def short_rows(r):
        for j in range(3):
            z = zf[j, r]
            z1 = jnp.where(lane >= 1, pltpu.roll(z, 1, 1), 0.0)
            z2 = jnp.where(lane >= 2, pltpu.roll(z, 2, 1), 0.0)
            k = 5 + 3 * j
            sf[j, r] = pcol_r[r, k : k + 1] * z + pcol_r[r, k + 1 : k + 2] * z1 + pcol_r[r, k + 2 : k + 3] * z2
        p = sf[2, r] * sf[1, r]
        pv[r] = p
        XS[r, 0:T], XS[r, T : 2 * T] = two(p)

    chunks(C, short_rows)
    spectrum(XSh, PS)
    zero = lax.broadcasted_iota(jnp.int32, (1, T), 1) == 0
    def prod(A, B, out, conj, low=None):
        @pl.loop(0, C // ROWS)
        def _(i):
            r = pl.ds(pl.multiple_of(i * ROWS, ROWS), ROWS)
            ar, ai = A[r, 0:T], A[r, T : 2 * T]
            br, bi = B[r, 0:T], B[r, T : 2 * T]
            ii = ai * bi
            iz = jnp.where(zero, 0.0, ii)
            if conj:
                re = ar * br + iz
                im = jnp.where(zero, ii, ar * bi - ai * br)
            else:
                re = ar * br - iz
                im = jnp.where(zero, ii, ar * bi + ai * br)
            for e, x in enumerate((re, im)):
                hi, lo = two(jnp.where(zero, 0.5 * x, x))
                out[r, e * T : e * T + T] = hi
                if low is not None:
                    low[pl.ds(r.start + e * C, ROWS)] = lo

    spread_step(0, 0, True)
    spread_step(0, 1)
    relay_on(1, 4)
    relay_on(1, 5)
    spread_step(1, 0)
    prod(KS, PS, XS, False, dzf)
    inverse(yv, dzf)

    def y_rows(r):
        y = yv[r] * (1.0 / T) + pcol_r[r, 16:17] * pv[r]
        yv[r] = y
        o = (y * sf[0, r]).astype(bf)
        for b in range(MP):
            oB[b, r] = o[:, TB * b : TB * b + TB]

    chunks(C, y_rows)
    c_o = [rc(oB.at[peer[k]], oK.at[m], pdev[k]) for k in (1, 2, 3)]
    oK[m] = oB[m]
    c_ct = [rc(cotB.at[peer[k]], cotK.at[m], pdev[k]) for k in (1, 2, 3)]
    cotK[m] = cotB[m]
    spread_step(1, 0, True)
    spread_step(1, 1)
    relay_on(2, 4)
    relay_on(2, 5)
    spread_step(2, 0)
    recv(c_wo2)

    recv(c_o)
    oks = oK[...].reshape(D, TB)
    for h in range(2):
        rv[h * H : (h + 1) * H, :] = dg(WO[h].reshape(D, H), oks, 0, 0)
    tot = jnp.zeros((1, TB), f32)
    for s in range(MP):
        rr = slice(s * C, s * C + C)
        r = rv[rr] + tokF[s, m].astype(f32) + COLS[rr, 4:5]
        rv[rr] = r
        tot = tot + jnp.sum(r, axis=0, keepdims=True)
    mu = tot * (1.0 / D)
    tot = jnp.zeros((1, TB), f32)
    for s in range(MP):
        xc = rv[s * C : s * C + C] - mu
        tot = tot + jnp.sum(xc * xc, axis=0, keepdims=True)
    sc2 = lax.rsqrt(tot * (1.0 / D) + epsilon)
    stat[2:3, 0:TB] = sc2
    for s in range(MP):
        rr = slice(s * C, s * C + C)
        xh = (rv[rr] - mu) * sc2
        xh2[rr] = xh
        n2P[rr, 0:TB] = (xh * COLS[rr, 2:3] + COLS[rr, 3:4]).astype(bf)
    c_n2 = rc(n2P.at[:, pl.ds(0, TB)], n2P.at[:, pl.ds(TB, TB)], dnb[0])

    recv(c_ct)
    for s in range(MP):
        goP[s * C : s * C + C, 0:TB] = (cotK[s].astype(f32) * wt[m, 0:1, :]).astype(bf)
    c_go = rc(goP.at[:, pl.ds(0, TB)], goP.at[:, pl.ds(TB, TB)], dnb[0])

    def ffn_slot(k):
        s = slot[k]
        for blk in (1, 0):
            l = slice(blk * TB, blk * TB + TB)
            a = dg(WU[s].reshape(D, H), n2P[:, l], 0, 0) + COLS[0:H, 64 + 8 * k : 65 + 8 * k]
            cdf = 0.5 * (1.0 + lax.erf(a * (1.0 / math.sqrt(2.0))))
            gv[k, :, l] = (a * cdf).astype(bf)
            gp = cdf + a * jnp.exp(-0.5 * a * a) * (1.0 / math.sqrt(2.0 * math.pi))
            da = dg(WD[s].reshape(H, D), goP[:, l], 1, 0) * gp
            dav[k, :, l] = da.astype(bf)
            rows = pl.ds(pl.multiple_of(H * x0, H), H)
            COLS[rows, 35 + k : 36 + k] += jnp.sum(da, axis=1, keepdims=True)

    def dn2_of(blk, out):
        l = slice(blk * TB, blk * TB + TB)
        for q in range(2):
            acc = dg(WU[m, q].reshape(H, H), dav[0, :, l], 1, 0)
            for k in range(1, MP):
                acc = acc + dg(WU[slot[k], q].reshape(H, H), dav[k, :, l], 1, 0)
            out[q * H : (q + 1) * H] = acc.astype(out.dtype)

    def br_of(blk, out):
        l = slice(blk * TB, blk * TB + TB)
        for q in range(0, D, H):
            acc = dg(WD[m, :, :, :, q : q + H].reshape(H, H), gv[0, :, l], 0, 0)
            for k in range(1, MP):
                acc = acc + dg(WD[slot[k], :, :, :, q : q + H].reshape(H, H), gv[k, :, l], 0, 0)
            out[q : q + H] = acc.astype(out.dtype)

    def ffn_grads(k):
        for h in range(2):
            gu = dg(n2P[h * H : (h + 1) * H], dav[k], 1, 1).astype(bf)
            gd = dg(gv[k, h * H // 2 : (h + 1) * H // 2], goP[...], 1, 1).astype(bf)
            for i in range(2):
                GU[k // 2, h, i, k % 2] = gu[i * QU : (i + 1) * QU, :]
                GD[k // 2, h, i, k % 2] = gd[i * QD : (i + 1) * QD, :]

    class Reduce:
        def __init__(self, order, G, R, X, FIN):
            self.x = [bits[o] for o in order]
            self.nb = [dnb[o] for o in order]
            self.n = len(order)
            self.G, self.R, self.X, self.FIN = G, R, X, FIN
            self.step = 0
            self.c = None

        def at(self, ref, k, flip=False):
            idx = list(self.x[:k])
            if flip:
                idx[-1] = 1 - idx[-1]
            return ref.at[tuple(idx)]

        def send(self):
            self.c = rc(self.at(self.G, self.step + 1, True), self.R[self.step], self.nb[self.step])

        def add(self):
            self.c.wait_recv()

            def one(g, r):
                if len(g.shape) > 2:
                    for a in range(g.shape[0]):
                        one(g.at[a], r.at[a])
                    return
                n = g.shape[0]

                def rows(q):
                    g[q] = (g[q].astype(f32) + r[q].astype(f32)).astype(bf)

                chunks(n, rows, 48)

            one(self.at(self.G, self.step + 1), self.R[self.step])
            self.step += 1

        def piece(self):
            return self.at(self.G, self.n)

        def extra(self):
            for e, b in enumerate(range(3, nbits)):
                bufs = self.X(e)
                parts = [self.piece()] if len(bufs) == 1 else [self.piece().at[pl.ds(2 * i, 2)] for i in range(2)]
                cs = [rc(p, x, dnb[b]) for p, x in zip(parts, bufs)]
                sent(cs)
                recv(cs)
                for p, x in zip(parts, bufs):
                    p[...] = (p[...].astype(f32) + x[...].astype(f32)).astype(bf)

        def gather(self):
            k = 2 * self.n - self.step
            ref = self.at(self.FIN, k)
            self.c = rc(ref, ref, self.nb[k - 1])
            self.step += 1

        def got(self):
            self.c.wait_recv()

    spare = lambda W, R, g: lambda e: [W.at[2 + e, g] if e < 2 else R]
    rU = [Reduce((1, 2), GU.at[g], [RU0.at[g], RU1.at[g]], spare(WU, RU1.at[g], g), FU.at[x0]) for g in range(2)]
    rD = [Reduce((2, 1), GD.at[g], [RD0.at[g], RD1.at[g]], spare(WD, RD1.at[g], g), FD.at[x0]) for g in range(2)]
    recv([c_go, c_n2])
    ffn_slot(0)
    spread_step(2, 0, True)
    spread_step(2, 1)
    spread_step(0, 1, True)
    ffn_slot(1)
    ffn_grads(0)
    ffn_grads(1)
    rU[0].send()
    rD[0].send()
    spread_step(1, 1, True)
    ffn_slot(2)
    spread_step(2, 1, True)
    ffn_slot(3)
    dn2_of(1, dnS)
    c_dn = rc(dnS, dnR, dnb[0])
    dn2_of(0, dnO)

    recv([c_dn])
    sent(c_ct)
    t1 = jnp.zeros((1, TB), f32)
    t2 = jnp.zeros((1, TB), f32)
    for s in range(MP):
        rr = slice(s * C, s * C + C)
        dn2 = dnO[rr] + dnR[rr].astype(f32)
        dnO[rr] = dn2
        xh = xh2[rr]
        dx = dn2 * xh
        COLS[rr, 33:34] = jnp.sum(dx, axis=1, keepdims=True)
        COLS[rr, 34:35] = jnp.sum(dn2, axis=1, keepdims=True)
        t1 = t1 + jnp.sum(dn2 * COLS[rr, 2:3], axis=0, keepdims=True)
        t2 = t2 + jnp.sum(dx * COLS[rr, 2:3], axis=0, keepdims=True)
    m1, m2 = t1 * (1.0 / D), t2 * (1.0 / D)
    for s in range(MP):
        rr = slice(s * C, s * C + C)
        dr = cotK[s].astype(f32) * wt[m, 0:1, :] + stat[2:3, 0:TB] * (dnO[rr] * COLS[rr, 2:3] - m1 - xh2[rr] * m2)
        COLS[rr, 32:33] = jnp.sum(dr, axis=1, keepdims=True)
        drS[s] = dr.astype(bf)
    drl = drS[...].reshape(D, TB)
    do = dg(WO[0].reshape(D, H), drl[0:H, :], 1, 0) + dg(WO[1].reshape(D, H), drl[H:D, :], 1, 0)
    doS[...] = do.astype(bf).reshape(MP, C, TB)
    c_do = [rc(doS.at[peer[k]], doB.at[m], pdev[k]) for k in (1, 2, 3)]
    doB[m] = doS[m]
    c_dr = [rc(drS.at[peer[k]], drB.at[m], pdev[k]) for k in (1, 2, 3)]
    drB[m] = drS[m]

    ffn_grads(2)
    ffn_grads(3)
    rU[1].send()
    rD[1].send()

    oks = oK[...].reshape(D, TB)
    rO = Reduce(ordO, GO, [RO0, RO1, RO2], lambda e: [WO.at[0, e]], FO)
    for s in range(MP):
        gw = dg(oK[s], drl, 1, 1).astype(bf)
        for i in range(8):
            GO[i // 4, (i // 2) % 2, i % 2, s * WR : (s + 1) * WR, :] = gw[
                WR * (i % 4) : WR * (i % 4) + WR, H * (i // 4) : H * (i // 4) + H
            ]
    rO.send()

    br_of(1, brS)
    c_br = rc(brS, brR, dnb[0])
    br_of(0, brO)

    @pl.when(m < MP - 1)
    def _():
        pl.semaphore_signal(gfree, inc=1, device_id=right, device_id_type=MESH)

    @pl.when(m > 0)
    def _():
        pl.semaphore_signal(gfree, inc=1, device_id=left, device_id_type=MESH)

    recv([c_br])
    sent(c_o)
    for s in range(MP):
        rr = slice(s * C, s * C + C)
        outS[s] = (rv[rr] + brO[rr] + brR[rr].astype(f32) + COLS[rr, 5:6]).astype(bf)
    rU[0].add()
    rU[0].send()
    rD[0].add()
    rD[0].send()
    rO.add()
    rO.send()

    recv(c_do)
    for b in range(MP):
        l = slice(TB * b, TB * b + TB)
        dO = doB[b].astype(f32)
        dyb = dO * sf[0, :, l]
        dsv[0, :, l] = dyb
        XS[:, l], XS[:, T + TB * b : T + TB * b + TB] = two(dyb)
        yv[:, l] = dO * yv[:, l]
    spectrum(XSh, dks)
    prod(KS, dks, XS, True)
    inverse(dsv.at[1])

    def back_rows(r):
        dy = dsv[0, r]
        SAc[r, 16:17] = jnp.sum(dy * pv[r], axis=1, keepdims=True)
        dgt = dsv[1, r] * (1.0 / T) + pcol_r[r, 16:17] * dy
        for j in range(3):
            ds = yv[r] if j == 0 else dgt * sf[3 - j, r]
            d1 = jnp.where(lane < T - 1, pltpu.roll(ds, T - 1, 1), 0.0)
            d2 = jnp.where(lane < T - 2, pltpu.roll(ds, T - 2, 1), 0.0)
            k = 5 + 3 * j
            dz = pcol_r[r, k : k + 1] * ds + pcol_r[r, k + 1 : k + 2] * d1 + pcol_r[r, k + 2 : k + 3] * d2
            dzf[pl.ds(r.start + j * C, ROWS)] = dz.astype(bf)
            SAc[r, 2 + j : 3 + j] = jnp.sum(dz, axis=1, keepdims=True)
            z = zf[j, r]
            SAc[r, k : k + 1] = jnp.sum(ds * z, axis=1, keepdims=True)
            SAc[r, k + 1 : k + 2] = jnp.sum(d1 * z, axis=1, keepdims=True)
            SAc[r, k + 2 : k + 3] = jnp.sum(d2 * z, axis=1, keepdims=True)

    chunks(C, back_rows)

    for step in range(3):
        for b in range(NC):
            sent_right = (m < MP - 1) if step == 0 else jnp.logical_and(m - step >= 0, m < MP - 1)
            sent_left = (m > 0) if step == 0 else jnp.logical_and(m + step < MP, m > 0)

            @pl.when(sent_right)
            def _():
                relay(0, step, b, m - step, right).wait_send()

            @pl.when(sent_left)
            def _():
                relay(1, step, b, m + step, left).wait_send()

    for step in range(3):
        for stage in range(2):
            spread_step(step, stage, "send")

    dn1S = tokF

    def dn1R(slot, b):
        return (gv if slot < 4 else dav).at[slot % 4 // 2 * 2 + b // 2, pl.ds(b % 2 * C, C), pl.ds(slot % 2 * TB, TB)]

    def rs_copy(way, s, b, dev, last=False):
        i = (way * MP + s) * MP + b
        return pltpu.make_async_remote_copy(
            src_ref=dn1S.at[s, b], dst_ref=dn1R(MP if last and way == 1 else s, b),
            send_sem=ss_rs.at[i], recv_sem=rs_rs.at[i], device_id=dev, device_id_type=MESH,
        )

    inner = jnp.logical_and(m > 0, m < MP - 1)

    @pl.when(inner)
    def _():
        pl.semaphore_wait(gfree, 2)

    @pl.when(jnp.logical_not(inner))
    def _():
        pl.semaphore_wait(gfree, 1)

    for b in range(MP):
        l = slice(TB * b, TB * b + TB)
        part = dg(winv[0], dzf[0:C, l], 0, 0)
        for j in (1, 2):
            part = part + dg(winv[j], dzf[j * C : (j + 1) * C, l], 0, 0)
        for s in (0, 3, 1, 2):
            own = part[s * C : (s + 1) * C]

            @pl.when(m == s)
            def _():
                dsv[0, :, l] = own

            @pl.when(m != s)
            def _():
                dn1S[s, b] = own.astype(bf)

            if s < MP - 1:
                @pl.when(m == MP - 1)
                def _():
                    rs_copy(1, s, b, left, s == MP - 2).start()
            if s > 0:
                @pl.when(m == 0)
                def _():
                    rs_copy(0, s, b, right).start()

    def rs_forward(b):
        for way, s in ((1, 0), (0, 3), (1, 1), (0, 2)):
            for mm in range(1, MP - 1):
                if (way == 1 and mm > s) or (way == 0 and mm < s):
                    last = mm - 1 == s if way == 1 else mm + 1 == s

                    @pl.when(m == mm)
                    def _():
                        rs_copy(way, s, b, left if way == 1 else right).wait_recv()
                        dn1S[s, b] = (dn1S[s, b].astype(f32) + dn1R(s, b)[...].astype(f32)).astype(bf)
                        rs_copy(way, s, b, left if way == 1 else right, last).start()

    rI = Reduce(ordO, GI, [RI0, RI1, RI2], lambda e: [XGI.at[e]], FI)
    PI = 3 * C // 4
    for h in range(2):
        gi = dg(dzf[h * 2 * PI : (h + 1) * 2 * PI, :], n1F[...], 1, 1).astype(bf)
        for i in range(2):
            for e in range(2):
                GI[e, h, i] = gi[i * PI : (i + 1) * PI, e * H : (e + 1) * H]
    rI.send()
    rs_forward(0)
    rU[1].add()
    rU[1].send()
    rD[1].add()
    rD[1].send()
    rs_forward(1)
    rU[0].add()
    rD[0].add()
    for e, b in enumerate(range(3, nbits)):
        pl.semaphore_signal(credit.at[e], inc=1, device_id=dnb[b], device_id_type=MESH)
    for e in range(nbits - 3):
        pl.semaphore_wait(credit.at[e], 1)
    rU[0].extra()
    rD[0].extra()
    c_z = {}

    def cross(k):
        for i, (r, Rz) in enumerate(((rU, RUz), (rD, RDz))):
            c_z[k, i] = rc(r[k // 2].piece().at[k % 2], Rz.at[k - 1], pdev[k])


    prod(PS, dks, XS, True, dzf)
    inverse(dsv.at[1], dzf)
    share = pen_coef / (D * dp_size)

    def filter_rows(r):
        kern = kv[r]
        k2 = kern * kern
        tail = jnp.sum(jnp.where(lane >= T // 2, k2, 0.0), axis=1, keepdims=True) * (2.0 / T)
        whole = jnp.sum(k2, axis=1, keepdims=True) * (1.0 / T) + 1e-06
        iw = 1.0 / whole
        ratio = tail * iw
        coef = jnp.where(lane >= T // 2, iw * (4.0 / T), 0.0) - ratio * iw * (2.0 / T)
        dkt = dsv[1, r] * (1.0 / T) + share * coef * kern
        SAc[r, 15:16] = -jnp.sum(dkt * kern * tramp, axis=1, keepdims=True)
        SAc[r, 18:19] = ratio
        draw = dkt * jnp.exp(-pcol_r[r, 15:16] * tramp)
        SAc[r, 14:15] = jnp.sum(draw, axis=1, keepdims=True)
        dsv[1, r] = draw

    chunks(C, filter_rows)
    rI.add()
    rI.send()
    rO.add()
    rO.send()
    rs_forward(2)
    h2 = h2s[...]
    h1 = h1s[...]
    w2 = u2s[...]
    w1 = u1s[...]
    draw = dsv[1]
    SM1[32 : 32 + FILT, :] = dg(h2, draw, 1, 1, precision=HI)
    dh2 = dg(f3_r[...], draw, 1, 0, precision=HI)
    e2 = dh2 * jnp.cos(q1s * w2)
    dw2 = e2 * q1s
    SM3[40 : 40 + FILT, :] = dg(h1, dw2, 1, 1, precision=HI)
    dh1 = dg(f2_r[...], dw2, 1, 0, precision=HI)
    e1 = dh1 * jnp.cos(q0 * w1)
    dw1 = e1 * q0
    SM3[0:40, :] = dg(emb[...], dw1, 1, 1, precision=HI)[0:40]
    fz[...] = jnp.zeros_like(fz)
    cols = (dw1, dw2, e1 * w1, e2 * w2)
    for i, col in enumerate(cols):
        fz[0:FILT, i : i + 1] = jnp.sum(col, axis=1, keepdims=True)
    fz[0:1, 4:5] = jnp.sum(SAc[:, 18:19], axis=0, keepdims=True) * (1.0 / (D * dp_size))
    SM3[40 + FILT : 48 + FILT, :] = fz[0:FILT, :].T[0:8, :]
    SM1[0:32, :] = SAc[...].T[0:32, :]
    SM2[...] = COLS[...].T[32:40, :]

    def hop(b, cur, got):
        cs = [rc(x, y.at[b], dnb[b]) for x, y in zip(cur, got)]

        def finish():
            recv(cs)
            for x, y in zip(cur, got):
                y[b] = y[b] + x[...]
            return [y.at[b] for y in got]

        return finish

    sm_got = (SM1r, SM2r, SM3r)
    hop_sm = hop(0, [SM1, SM2, SM3], sm_got)
    rU[1].add()
    rD[1].add()
    for e, b in enumerate(range(3, nbits)):
        pl.semaphore_signal(credit.at[e], inc=1, device_id=dnb[b], device_id_type=MESH)
    for e in range(nbits - 3):
        pl.semaphore_wait(credit.at[e], 1)
    rU[1].extra()
    rD[1].extra()
    for mm, way in ((0, 0), (MP - 1, 1)):
        @pl.when(m == mm)
        def _():
            for b in range(MP):
                for s in range(MP):
                    if s != mm:
                        rs_copy(way, s, b, right if way == 0 else left).wait_send()

    for k in (1, 2, 3):
        cross(k)

    rs_forward(3)
    rO.add()
    rO.extra()
    c_zo = [rc(rO.piece().at[pl.ds(WR * peer[k], WR)], RO3.at[k - 1], pdev[k]) for k in (1, 2, 3)]
    rI.add()
    rI.send()

    rI.add()
    rI.extra()
    FI[x0, x1, x2] = rI.piece()[...]
    rI.gather()

    cur = hop_sm()
    hop_sm = hop(1, cur, sm_got)

    for mm in range(MP):
        @pl.when(m == mm)
        def _():
            for b in range(MP):
                l = slice(TB * b, TB * b + TB)
                if mm < MP - 1:
                    rs_copy(1, mm, b, left, True).wait_recv()
                    dsv[0, :, l] += dn1R(MP, b)[...].astype(f32)
                if mm > 0:
                    rs_copy(0, mm, b, right).wait_recv()
                    dsv[0, :, l] += dn1R(mm, b)[...].astype(f32)

    dn1 = dsv[0]
    q1 = dn1 * pcol_r[:, 0:1]
    for b in range(MP):
        l = slice(TB * b, TB * b + TB)
        xhb = (tokF[m, b].astype(f32) - stat[0:1, l]) * stat[1:2, l]
        yv[:, l] = xhb
    xh1 = yv[...]
    stS[0:1, :] = jnp.sum(q1, axis=0, keepdims=True)
    stS[1:2, :] = jnp.sum(q1 * xh1, axis=0, keepdims=True)
    c_st = [rc(stS, stR.at[k - 1], pdev[k]) for k in (1, 2, 3)]
    SM4[...] = jnp.zeros_like(SM4)
    SAc[:, 0:1] = jnp.sum(dn1 * xh1, axis=1, keepdims=True)
    SAc[:, 1:2] = jnp.sum(dn1, axis=1, keepdims=True)
    SM4[...] = SAc[...].T[0:8, :]
    h4 = hop(0, [SM4], [SM4r])
    c_out = [rc(outS.at[peer[k]], outB.at[m], pdev[k]) for k in (1, 2, 3)]
    outB[m] = outS[m]
    for b in range(2, nbits):
        cur = hop_sm()
        hop_sm = hop(b, cur, sm_got)
    rI.got()
    rI.gather()
    recv(c_zo + list(c_z.values()))
    for r, Rz in ((rU[0], RUz), (rD[0], RDz)):
        own = r.piece()[0].astype(f32)
        for k in range(3):
            own = own + Rz[k].astype(f32)
        r.FIN[r.x[0], r.x[1]] = own.astype(bf)
        r.gather()
    own = rO.piece()[pl.ds(WR * m, WR), :].astype(f32)
    for k in range(3):
        own = own + RO3[k].astype(f32)
    FO[x0, x1, x2] = own.astype(bf)
    rO.gather()
    recv(c_st)
    tot = stS[0:2, :]
    for k in range(3):
        tot = tot + stR[k, 0:2, :]
    recv(c_dr)
    for b in range(MP):
        l = slice(TB * b, TB * b + TB)
        back = stat[1:2, l] * (q1[:, l] - tot[0:1, l] * (1.0 / D) - xh1[:, l] * (tot[1:2, l] * (1.0 / D)))
        dsv[1, :, l] = drB[b].astype(f32) + back
    c_dtok = lc(dsv.at[1], dtok_o)
    SM1, SM2, SM3 = hop_sm()
    c_s1 = [rc(SM3, SMz3.at[k - 1], pdev[k]) for k in (1, 2, 3)]
    c_s2 = [rc(SM2, SMz2.at[k - 1], pdev[k]) for k in (1, 2, 3)]

    cur4 = h4()
    h4 = hop(1, cur4, [SM4r])
    rU[0].got()
    rU[0].gather()
    rD[0].got()
    rD[0].gather()
    rI.got()
    rI.gather()
    rO.got()
    rO.gather()
    for b in range(2, nbits):
        cur4 = h4()
        h4 = hop(b, cur4, [SM4r])
    recv(c_out)
    c_outh = lc(outB, outb_o)
    recv(c_s1)
    recv(c_s2)
    sm1_o[...] = SM1[...]
    a3 = SM3[...]
    for k in range(3):
        a3 = a3 + SMz3[k]
    sm3_o[...] = a3
    a2 = SM2[...]
    for k in range(3):
        a2 = a2 + SMz2[k]
    dbu = SM2[3:4, :]
    for k in range(3):
        dbu = dbu + SMz2[k, 4 + k : 5 + k, :]
    sm2_o[...] = jnp.broadcast_to(dbu, (8, D))
    for mm in range(MP):
        @pl.when(m == mm)
        def _():
            sm4_o[2:5, :] = a2[0:3, mm * C : (mm + 1) * C]
    rU[0].got()
    rD[0].got()
    c_fu = rc(FU.at[x0], FU.at[x0], dnb[0])
    c_fd = rc(FD.at[x0], FD.at[x0], dnb[0])
    outs = [lc(FU.at[x0], gup_o.at[x0]), lc(FD.at[x0], gdn_o.at[x0])]
    rO.got()
    rO.gather()
    rI.got()
    outs.append(lc(FI, gin_o))
    cur4 = h4()
    sm4_o[0:2, :] = cur4[0][0:2, :]
    recv([c_fu, c_fd])
    outs += [lc(FU.at[1 - x0], gup_o.at[1 - x0]), lc(FD.at[1 - x0], gdn_o.at[1 - x0])]
    rO.got()
    outs.append(lc(FO, gwo_o))
    for c in outs + [c_dtok, c_outh]:
        c.wait()

    for c in pending:
        c.wait_send()
    for s in range(MP):
        if s < MP - 1:
            @pl.when(jnp.logical_and(m > s, m < MP - 1))
            def _():
                for b in range(MP):
                    rs_copy(1, s, b, left).wait_send()
        if s > 0:
            @pl.when(jnp.logical_and(m < s, m > 0))
            def _():
                for b in range(MP):
                    rs_copy(0, s, b, right).wait_send()


def finish_kernel(
    outb, dtok, gup, gdn, gwo, gin, sm1, sm2, sm3, sm4,
    out_o, dtok_o, dg1, ds1, dwin_o, dbin, dtaps, df1, dc1, df2, dc2, dsq, df3, dc3, ddec, dcb,
    dwout_o, dbo, dg2, ds2, dwup_o, dbu, dwdn_o, dbd, pen,
    vout, vdt, vup, vdn, vwo, vin, fout, fup, fdn, fwo, fin, isem, osem,
):
    MPN, C, TB = vout.shape
    ins = [(outb, vout), (dtok, vdt), (gup, vup), (gdn, vdn), (gwo, vwo), (gin, vin)]
    cin = [pltpu.make_async_copy(a, b, isem.at[i]) for i, (a, b) in enumerate(ins)]
    for i in (2, 3, 0, 1, 5, 4):
        cin[i].start()
    cout = []

    def put(src, dst):
        c = pltpu.make_async_copy(src, dst, osem.at[len(cout)])
        c.start()
        cout.append(c)

    PR, D = vdn.shape[3:]
    H = D // 2
    cin[2].wait()
    for e in range(2):
        fup[:, e * H : (e + 1) * H] = vup[e].reshape(D, H).astype(f32)
    put(fup, dwup_o)
    cin[3].wait()
    for e in range(2):
        fdn[e * H : (e + 1) * H, :] = vdn[e].reshape(H, D).astype(f32)
        put(fdn.at[pl.ds(e * H, H)], dwdn_o.at[pl.ds(e * H, H)])
    cin[0].wait()
    for b in range(MPN):
        fout[:, TB * b : TB * b + TB] = vout[b].astype(f32)
    put(fout, out_o)
    cin[1].wait()
    put(vdt, dtok_o)
    cin[5].wait()
    for e in range(2):
        fin[:, e * H : (e + 1) * H] = vin[e].reshape(3 * C, H).astype(f32)
    put(fin, dwin_o)
    cin[4].wait()
    for e in range(2):
        fwo[:, e * H : (e + 1) * H] = vwo[e].reshape(C, H).astype(f32)
    put(fwo, dwout_o)
    for o, r in ((dg1, sm4[0:1]), (ds1, sm4[1:2]), (dbo, sm4[2:3]), (dg2, sm4[3:4]), (ds2, sm4[4:5]),
                 (dc3, sm1[14:15]), (ddec, sm1[15:16]), (dcb, sm1[16:17]), (dbd, sm1[17:18])):
        o[...] = r.reshape(C)
    dbu[...] = sm2[0:1].reshape(D)
    dbin[...] = sm1[2:5]
    for j in range(3):
        dtaps[j] = sm1[5 + 3 * j : 8 + 3 * j]
    df3[...] = sm1[32 : 32 + FILT]
    df1[...] = sm3[0:EMB]
    df2[...] = sm3[40 : 40 + FILT]
    dc1[...] = sm3[40 + FILT : 41 + FILT].reshape(FILT)
    dc2[...] = sm3[41 + FILT : 42 + FILT].reshape(FILT)
    dsq[...] = sm3[42 + FILT : 44 + FILT]
    pen[...] = sm3[44 + FILT : 45 + FILT, 0:1]
    for c in cout:
        c.wait()


def build(dp_size):
    nbits = int(math.log2(dp_size))

    def per_device(
        tokens, cotangent, seg_ids, row_lengths, group_tags, group_weights, gain_one, shift_one,
        w_in, b_in, taps, f_one, c_one, f_two, c_two, sine_freq, f_three, c_three, decay, conv_bias,
        w_out, b_out, gain_two, shift_two, w_up, b_up, w_down, b_down,
    ):
        T, C = tokens.shape
        D = C * MP
        TB = T // MP
        fwd, emb = tables(T)
        V = pltpu.VMEM
        PR, WR, H, PI = D // 8, C // 4, D // 2, 3 * C // 4
        ne = max(nbits - 3, 1)
        scratch = dict(
            tokF=V((MP, MP, C, TB), bf), cotB=V((MP, C, TB), bf),
            cotK=V((MP, C, TB), bf), n1F=V((D, T), bf), winv=V((3, C, D), bf), F=V((T, 2 * T), bf),
            emb=V((128, T), f32), zf=V((3, C, T), f32), sf=V((3, C, T), f32),
            yv=V((C, T), f32), pv=V((C, T), f32), kv=V((C, T), f32), KS=V((C, 2 * T), f32),
            PS=V((C, 2 * T), f32), XS=V((C, 2 * T), bf),
            oB=V((MP, C, TB), bf), oK=V((MP, C, TB), bf), WO=V((2, MP, C, H), bf), WU=V((MP, 2, 2, D // 4, H), bf), WD=V((MP, 2, 2, PR, D), bf),
            rv=V((D, TB), f32), xh2=V((D, TB), f32), n2P=V((D, 2 * TB), bf), goP=V((D, 2 * TB), bf),
            gv=V((MP, H, 2 * TB), bf), dav=V((MP, H, 2 * TB), bf), wt=V((MP, 8, TB), f32), stat=V((8, T), f32),
            PG=V((MP, 8, C), f32), COLS=V((D, 128), f32),
            brS=V((D, TB), bf), brR=V((D, TB), bf), dnS=V((D, TB), bf), dnR=V((D, TB), bf),
            outB=V((MP, C, TB), bf), drB=V((MP, C, TB), bf),
            doS=V((MP, C, TB), bf), doB=V((MP, C, TB), bf), dnO=V((D, TB), f32), brO=V((D, TB), f32),
            GU=V((2, 2, 2, 2, D // 4, H), bf), RU0=V((2, 2, 2, D // 4, H), bf), RU1=V((2, 2, D // 4, H), bf), RUz=V((3, D // 4, H), bf),
            GD=V((2, 2, 2, 2, PR, D), bf), RD0=V((2, 2, 2, PR, D), bf), RD1=V((2, 2, PR, D), bf), RDz=V((3, PR, D), bf),
            GO=V((2, 2, 2, C, H), bf), RO0=V((2, 2, C, H), bf), RO1=V((2, C, H), bf), RO2=V((C, H), bf),
            RO3=V((3, WR, H), bf), FO=V((2, 2, 2, WR, H), bf),
            GI=V((2, 2, 2, PI, H), bf), RI0=V((2, 2, PI, H), bf), RI1=V((2, PI, H), bf), RI2=V((PI, H), bf),
            FI=V((2, 2, 2, PI, H), bf),
            dzf=V((3 * C, T), bf),
            stS=V((8, T), f32), stR=V((3, 8, T), f32), SAc=V((C, 128), f32),
            SM1=V((96, C), f32), SM1r=V((nbits, 96, C), f32), SM3=V((48 + FILT, FILT), f32), SM3r=V((nbits, 48 + FILT, FILT), f32), SM2=V((8, D), f32), SM2r=V((nbits, 8, D), f32),
            SMz3=V((3, 48 + FILT, FILT), f32), SMz2=V((3, 8, D), f32), SM4=V((8, C), f32), SM4r=V((nbits, 8, C), f32),
            XGI=V((ne, PI, H) if nbits > 3 else (1, 16, 128), bf),
            h1s=V((FILT, T), f32), h2s=V((FILT, T), f32), u1s=V((FILT, T), f32), u2s=V((FILT, T), f32),
            dks=V((C, 2 * T), f32), dsv=V((2, C, T), f32), prow=V((32, C), f32), pcol_r=V((C, 32), f32), bup=V((MP, 8, H), f32), fz=V((128, FILT), f32), frow=V((8, FILT), f32),
            gfree=pltpu.SemaphoreType.REGULAR, credit=pltpu.SemaphoreType.REGULAR((ne,)), ssem=pltpu.SemaphoreType.DMA((NSEM,)), rsem=pltpu.SemaphoreType.DMA((NSEM,)),
            lsem=pltpu.SemaphoreType.DMA((40,)), ss_tok=pltpu.SemaphoreType.DMA((36,)), rs_tok=pltpu.SemaphoreType.DMA((36,)),
            ss_rs=pltpu.SemaphoreType.DMA((32,)), rs_rs=pltpu.SemaphoreType.DMA((32,)), ss_sp=pltpu.SemaphoreType.DMA((24,)), rs_sp=pltpu.SemaphoreType.DMA((24,)),
        )
        anyspec = pl.BlockSpec(memory_space=pl.ANY)
        vm = pl.BlockSpec(memory_space=pltpu.VMEM)
        sm = pl.BlockSpec(memory_space=pltpu.SMEM)
        S = jax.ShapeDtypeStruct
        outs = pl.pallas_call(
            functools.partial(main_kernel, nbits, dp_size, (T, C, D)),
            out_shape=[
                S((MP, C, TB), bf), S((C, T), f32), S((2, 2, 2, D // 4, H), bf), S((2, 2, 2, PR, D), bf),
                S((2, 2, 2, WR, H), bf), S((2, 2, 2, PI, H), bf), S((96, C), f32), S((8, D), f32),
                S((48 + FILT, FILT), f32), S((8, C), f32),
            ],
            in_specs=[anyspec] * 8 + [vm, sm, sm, sm] + [vm] * 18,
            out_specs=[anyspec] * 6 + [vm] * 4,
            scratch_shapes=list(scratch.values()),
            compiler_params=pltpu.CompilerParams(
                collective_id=0, has_side_effects=True, vmem_limit_bytes=63 * 2**20
            ),
            name="hyena_block",
        )(
            tokens.T, cotangent.T, jnp.transpose(w_in, (0, 2, 1)), w_out, w_up, w_down, jnp.asarray(fwd), jnp.asarray(emb),
            seg_ids, row_lengths, group_tags, group_weights, gain_one, shift_one, b_in, taps, f_one, c_one,
            f_two, c_two, sine_freq, f_three, c_three, decay, conv_bias, b_out, gain_two, shift_two, b_up, b_down,
        )
        v1, vF, v2 = S((C,), f32), S((FILT,), f32), S((2, FILT), f32)
        res = pl.pallas_call(
            finish_kernel,
            out_shape=[
                S((C, T), f32), S((C, T), f32), v1, v1, S((3 * C, D), f32), S((3, C), f32), S((3, 3, C), f32),
                S((EMB, FILT), f32), vF, S((FILT, FILT), f32), vF, v2, S((FILT, C), f32), v1, v1, v1,
                S((C, D), f32), v1, v1, v1, S((D, D), f32), S((D,), f32), S((D, D), f32), v1, S((1, 1), f32),
            ],
            in_specs=[anyspec] * 6 + [vm] * 4,
            out_specs=[anyspec if i in (0, 1, 4, 16, 20, 22) else vm for i in range(25)],
            scratch_shapes=[
                V((MP, C, TB), bf), V((C, T), f32), V((2, 2, 2, D // 4, H), bf), V((2, 2, 2, PR, D), bf), V((2, 2, 2, WR, H), bf),
                V((2, 2, 2, PI, H), bf), V((C, T), f32), V((D, D), f32), V((D, D), f32), V((C, D), f32), V((3 * C, D), f32),
                pltpu.SemaphoreType.DMA((6,)), pltpu.SemaphoreType.DMA((8,)),
            ],
            compiler_params=pltpu.CompilerParams(vmem_limit_bytes=63 * 2**20),
            name="hyena_finish",
        )(*outs)
        res = list(res)
        res[0], res[1] = res[0].T, res[1].T
        res[4] = jnp.transpose(res[4].reshape(3, C, D), (0, 2, 1))
        res[24] = res[24].reshape(())
        return tuple(res)

    return per_device


def solution(mesh):
    placed = (
        P("dp", "mp"), P("dp", "mp"), P("dp", None), P("dp"), P("dp", None), P(), P("mp"), P("mp"),
        P(None, None, "mp"), P(None, "mp"), P(None, None, "mp"), P(), P(), P(), P(), P(),
        P(None, "mp"), P("mp"), P("mp"), P("mp"), P("mp", None), P("mp"), P("mp"), P("mp"),
        P(None, "mp"), P("mp"), P("mp", None), P("mp"),
    )
    out_specs = (
        P("dp", "mp"), P("dp", "mp"), P("mp"), P("mp"), P(None, None, "mp"), P(None, "mp"),
        P(None, None, "mp"), P(), P(), P(), P(), P(), P(None, "mp"), P("mp"), P("mp"), P("mp"),
        P("mp", None), P("mp"), P("mp"), P("mp"), P(None, "mp"), P("mp"), P("mp", None), P("mp"), P(),
    )
    return jax.shard_map(
        build(mesh.shape["dp"]), mesh=mesh, in_specs=placed, out_specs=out_specs, check_vma=False
    )
```

```python
import functools
import math

import jax
import jax.numpy as jnp
import ml_dtypes
import numpy as np
from jax import lax
from jax.experimental import pallas as pl
from jax.experimental.pallas import tpu as pltpu
from jax.sharding import PartitionSpec as P

EMB = 33
SEGS = 4
GROUPS = 4
FILT = 64
MP = 4
epsilon = 1e-05
pen_coef = 0.5
HI = lax.Precision.HIGHEST
MESH = pl.DeviceIdType.MESH
bf = jnp.bfloat16
f32 = jnp.float32
NSEM = 200


def dg(left, right, left_dim, right_dim, **kw):
    return lax.dot_general(
        left, right, (((left_dim,), (right_dim,)), ((), ())), preferred_element_type=f32, **kw
    )


def tables(seq):
    t = np.arange(seq)
    ang = (np.outer(t, t) % (2 * seq)) * (2.0 * np.pi / (2 * seq))
    cos, sin = np.cos(ang), np.sin(ang)
    fwd = np.concatenate([cos, -sin], axis=1)
    alt = np.where(t % 2 == 0, 1.0, -1.0)
    fwd[:, seq] = alt
    emb = np.zeros((128, seq))
    emb[0] = t / seq
    for m in range(1, (EMB - 1) // 2 + 1):
        a = (t * m % seq) * (2.0 * np.pi / seq)
        emb[m] = np.cos(a)
        emb[(EMB - 1) // 2 + m] = np.sin(a)
    low = lambda v: v.astype(np.float32).astype(ml_dtypes.bfloat16)
    return low(fwd), emb.astype(np.float32)


def main_kernel(
    nbits, dp_size, dims,
    tok_h, cot_h, win_h, wout_h, wup_h, wdn_h, F_h, emb_h,
    seg_r, len_r, tag_r, gw_r, g1_r, s1_r, bin_r, taps_r, f1_r, c1_r, f2_r, c2_r, sq_r, f3_r, c3_r,
    dec_r, cb_r, bo_r, g2_r, s2_r, bu_r, bd_r,
    outb_o, dtok_o, gup_o, gdn_o, gwo_o, gin_o, sm1_o, sm2_o, sm3_o, sm4_o,
    tokF, cotB, cotK, n1F, winv, F, emb, zf, sf, yv, pv, kv, KS, PS, XS,
    oB, oK, WO, WU, WD, rv, xh2, n2P, goP, gv, dav, wt, stat, PG, COLS,
    brS, brR, dnS, dnR, outB, drB, doS, doB, dnO, brO,
    GU, RU0, RU1, RUz, GD, RD0, RD1, RDz, GO, RO0, RO1, RO2, RO3, FO,
    GI, RI0, RI1, RI2, FI, dzf, stS, stR, SAc, SM1, SM1r, SM3, SM3r, SM2, SM2r, SMz3, SMz2,
    SM4, SM4r, XGI, h1s, h2s, u1s, u2s, dks, dsv, prow, pcol_r, bup, fz, frow,
    gfree, credit, ssem, rsem, lsem, ss_tok, rs_tok, ss_rs, rs_rs, ss_sp, rs_sp,
):
    T, C, D = dims
    TB = T // MP
    d = lax.axis_index("dp")
    m = lax.axis_index("mp")
    bits = [(d // 2**b) % 2 for b in range(nbits)]
    dnb = [(d + (1 - 2 * bits[b]) * 2**b, m) for b in range(nbits)]
    peer = {1: m + 1 - 2 * (m % 2), 2: (m + 2) % 4, 3: 3 - m}
    pdev = {k: (d, peer[k]) for k in peer}
    slot = [m, peer[1], peer[2], peer[3]]
    used = [0]
    pending = []

    def rc(src, dst, dev):
        i = used[0]
        used[0] += 1
        c = pltpu.make_async_remote_copy(
            src_ref=src, dst_ref=dst, send_sem=ssem.at[i], recv_sem=rsem.at[i],
            device_id=dev, device_id_type=MESH,
        )
        c.start()
        pending.append(c)
        return c

    lused = [0]

    def lc(src, dst):
        i = lused[0]
        lused[0] += 1
        c = pltpu.make_async_copy(src, dst, lsem.at[i])
        c.start()
        return c

    def recv(cs):
        for c in cs:
            c.wait_recv()

    FU, FD = WU, WD
    H = D // 2
    QU, QD = D // 4, D // 8
    x0, x1, x2 = bits[0], bits[1], bits[2]
    xU, xD = (x1, x2), (x2, x1)
    pU, pD = 2 * x1 + x2, 2 * x2 + x1
    outS, drS = oB, cotB

    def sent(cs):
        for c in cs:
            c.wait_send()
            pending[:] = [p for p in pending if p is not c]

    c_tok = [lc(tok_h.at[:, pl.ds(TB * b, TB)], tokF.at[m, b]) for b in range(MP)]
    c_cot = [lc(cot_h.at[:, pl.ds(TB * b, TB)], cotB.at[b]) for b in range(MP)]
    c_wo = [lc(wout_h.at[:, pl.ds(h * (D // 2), D // 2)], WO.at[h, m]) for h in range(2)]
    c_win = lc(win_h, winv)
    c_emb = lc(emb_h, emb)
    c_F = lc(F_h, F)
    half = pl.ds(pl.multiple_of(H * x0, H), H)
    c_own = []
    for p in range(4):
        c_own.append(lc(wup_h.at[pl.ds(QU * p, QU), half], WU.at[m, p // 2, p % 2]))
        c_own.append(lc(wdn_h.at[pl.ds(pl.multiple_of(H * x0 + QD * p, QD), QD)], WD.at[m, p // 2, p % 2]))

    barrier = pltpu.get_barrier_semaphore()
    for dev in list(pdev.values()) + dnb:
        pl.semaphore_signal(barrier, inc=1, device_id=dev, device_id_type=MESH)
    pl.semaphore_wait(barrier, 3 + nbits)

    right = (d, lax.rem(m + 1, MP))
    left = (d, lax.rem(m + MP - 1, MP))
    NC = MP + 2

    def relay(way, step, chunk, shard, dev):
        i = (way * 3 + step) * NC + chunk
        if chunk == 4:
            ref = WU.at[shard, xU[0], xU[1]]
        elif chunk == 5:
            ref = WD.at[shard, xD[0], xD[1]]
        else:
            ref = tokF.at[shard, chunk]
        return pltpu.make_async_remote_copy(
            src_ref=ref, dst_ref=ref, send_sem=ss_tok.at[i], recv_sem=rs_tok.at[i],
            device_id=dev, device_id_type=MESH,
        )

    def relay_own(chunk):
        @pl.when(m < MP - 1)
        def _():
            relay(0, 0, chunk, m, right).start()

        @pl.when(m > 0)
        def _():
            relay(1, 0, chunk, m, left).start()

    def relay_on(step, chunk):
        @pl.when(m - 1 - step >= 0)
        def _():
            relay(0, step, chunk, m - 1 - step, right).wait_recv()

        @pl.when(m + 1 + step < MP)
        def _():
            relay(1, step, chunk, m + 1 + step, left).wait_recv()

        if step < 2:
            @pl.when(jnp.logical_and(m - 1 - step >= 0, m < MP - 1))
            def _():
                relay(0, step + 1, chunk, m - 1 - step, right).start()

            @pl.when(jnp.logical_and(m + 1 + step < MP, m > 0))
            def _():
                relay(1, step + 1, chunk, m + 1 + step, left).start()

    for b in range(MP):
        c_tok[b].wait()
        relay_own(b)

    for i, ref in enumerate((g1_r, s1_r, g2_r, s2_r, bo_r, bd_r)):
        PG[m, i : i + 1, :] = ref[...].reshape(1, C)
    brow = bu_r[...].reshape(1, D)
    bup[m] = jnp.zeros((8, H), f32)
    bup[m, 0:1, :] = jnp.where(x0 == 0, brow[:, 0:H], brow[:, H:D])
    c_pg = [rc(PG.at[m], PG.at[m], pdev[k]) for k in (1, 2, 3)]
    c_pg += [rc(bup.at[m], bup.at[m], pdev[k]) for k in (1, 2, 3)]

    for c in c_wo:
        c.wait()
    WR = C // 4
    ordO = (0, 1, 2)

    def wo_send(rows, dev):
        return [rc(WO.at[x0, peer[k], rows], WO.at[x0, peer[k], rows], dev) for k in (1, 2, 3)]

    WR1 = pl.ds(WR * (2 * x1 + x2), WR)
    c_wop = [rc(WO.at[x0, m, WR1], WO.at[x0, m, WR1], pdev[k]) for k in (1, 2, 3)]

    def spread(way, step, stage, wait=False):
        shard = m - 1 - step if way == 0 else m + 1 + step

        @pl.when(shard >= 0 if way == 0 else shard < MP)
        def _():
            for e, (W, x, nb) in enumerate(((WU, xU, (dnb[2], dnb[1])), (WD, xD, (dnb[1], dnb[2])))):
                ref = W.at[shard, x[0], x[1]] if stage == 0 else W.at[shard, x[0]]
                i = ((way * 3 + step) * 2 + stage) * 2 + e
                c = pltpu.make_async_remote_copy(
                    src_ref=ref, dst_ref=ref, send_sem=ss_sp.at[i], recv_sem=rs_sp.at[i],
                    device_id=nb[stage], device_id_type=MESH,
                )
                if wait == "send":
                    c.wait_send()
                elif wait:
                    c.wait_recv()
                else:
                    c.start()

    def spread_step(step, stage, wait=False):
        for way in range(2):
            spread(way, step, stage, wait)

    seg = seg_r[...]
    tag = jnp.zeros((1, T), jnp.int32)
    for s in range(SEGS):
        tag = jnp.where(seg == s, tag_r[0, s], tag)
    wi = jnp.zeros((1, T), jnp.int32)
    for g in range(GROUPS):
        wi = jnp.where(tag == g, gw_r[g], wi)
    place = lax.broadcasted_iota(jnp.int32, (1, T), 1)
    wi = jnp.where(place < len_r[0], wi, 0)
    wf = wi.astype(f32)
    for b in range(MP):
        wt[b, 0:1, :] = wf[:, TB * b : TB * b + TB]

    relay_on(0, 0)

    prow[...] = jnp.zeros_like(prow)
    for i, ref in ((0, g1_r), (1, s1_r), (14, c3_r), (15, dec_r), (16, cb_r)):
        prow[i : i + 1, :] = ref[...].reshape(1, C)
    prow[2:5, :] = bin_r[...]
    for j in range(3):
        prow[5 + 3 * j : 8 + 3 * j, :] = taps_r[j]
    pcol_r[...] = prow[...].T

    SAc[...] = jnp.zeros_like(SAc)
    dbd = jnp.zeros((C, 1), f32)
    for b in range(MP):
        c_cot[b].wait()
        dbd = dbd + jnp.sum(cotB[b].astype(f32) * wf[:, TB * b : TB * b + TB], axis=1, keepdims=True)
    SAc[:, 17:18] = dbd
    COLS[...] = jnp.zeros_like(COLS)

    relay_on(0, 1)

    ROWS = 48

    def chunks(n, fn, step=ROWS):
        @pl.loop(0, n // step)
        def _(i):
            fn(pl.ds(pl.multiple_of(i * step, step), step))

    NB = 512

    def spectrum(parts, out):
        for n in range(0, 2 * T, NB):
            acc = dg(parts[0][...], F[:, n : n + NB], 1, 0)
            for part in parts[1:]:
                acc = acc + dg(part[...], F[:, n : n + NB], 1, 0)
            out[:, n : n + NB] = acc

    def inverse(out, low=None):
        for n in range(0, T, NB // 2):
            rows = slice(n, n + NB // 2)
            acc = dg(XS[...], F[rows, :], 1, 1)
            if low is not None:
                for e in range(2):
                    acc = acc + dg(low[e * C : (e + 1) * C], F[rows, e * T : e * T + T], 1, 1)
            out[:, rows] = acc

    def two(x):
        hi = x.astype(bf)
        return hi, (x - hi.astype(f32)).astype(bf)

    tramp = place.astype(f32) * (1.0 / T)
    fz[...] = jnp.zeros_like(fz)
    fz[0:EMB, :] = f1_r[...]
    frow[...] = jnp.zeros_like(frow)
    frow[0:1, :] = c1_r[...].reshape(1, FILT)
    frow[1:2, :] = c2_r[...].reshape(1, FILT)
    frow[2:4, :] = sq_r[...]
    fcol = frow[...].T
    c1, c2, q0, q1s = (fcol[:, i : i + 1] for i in range(4))
    c_emb.wait()
    w1 = dg(fz[...], emb[...], 0, 0, precision=HI) + c1
    u1s[...] = w1
    h1 = jnp.sin(q0 * w1)
    h1s[...] = h1
    w2 = dg(f2_r[...], h1, 0, 0, precision=HI) + c2
    u2s[...] = w2
    h2 = jnp.sin(q1s * w2)
    h2s[...] = h2
    relay_on(0, 2)
    kv[...] = dg(f3_r[...], h2, 0, 0, precision=HI)

    def kern_rows(r):
        k = (kv[r] + pcol_r[r, 14:15]) * jnp.exp(-pcol_r[r, 15:16] * tramp)
        kv[r] = k
        XS[r, 0:T], XS[r, T : 2 * T] = two(k)

    chunks(C, kern_rows)
    relay_on(0, 3)
    c_F.wait()
    XSh = [XS.at[:, pl.ds(0, T)], XS.at[:, pl.ds(T, T)]]
    spectrum(XSh, KS)

    recv(c_wop)
    c_wo2 = wo_send(WR1, dnb[2])
    for b in range(MP):
        relay_on(1, b)
    for c in c_own:
        c.wait()
    relay_own(4)
    relay_own(5)
    recv(c_wo2)
    c_wo2 = wo_send(pl.ds(2 * WR * x1, 2 * WR), dnb[1])

    recv(c_pg)
    for s in range(MP):
        COLS[s * C : (s + 1) * C, 0:8] = PG[s].T
    for k in range(MP):
        COLS[0:H, 64 + 8 * k : 72 + 8 * k] = bup[slot[k]].T

    c_win.wait()

    def norm_block(b):
        tot = jnp.zeros((1, TB), f32)
        for s in range(MP):
            tot = tot + jnp.sum(tokF[s, b].astype(f32), axis=0, keepdims=True)
        mu = tot * (1.0 / D)
        tot = jnp.zeros((1, TB), f32)
        for s in range(MP):
            xc = tokF[s, b].astype(f32) - mu
            tot = tot + jnp.sum(xc * xc, axis=0, keepdims=True)
        sc = lax.rsqrt(tot * (1.0 / D) + epsilon)
        for s in range(MP):
            r = slice(s * C, s * C + C)
            xh = (tokF[s, b].astype(f32) - mu) * sc
            n1F[r, TB * b : TB * b + TB] = (xh * COLS[r, 0:1] + COLS[r, 1:2]).astype(bf)
        n1 = n1F[:, TB * b : TB * b + TB]
        stat[0:1, TB * b : TB * b + TB] = mu
        stat[1:2, TB * b : TB * b + TB] = sc
        for j in range(3):
            zf[j, :, TB * b : TB * b + TB] = dg(winv[j], n1, 1, 0) + pcol_r[:, 2 + j : 3 + j]

    for b in range(MP):
        relay_on(2, b)
        norm_block(b)
    recv(c_wo2)
    c_wo2 = wo_send(pl.ds(0, C), dnb[0])
    relay_on(0, 4)
    relay_on(0, 5)
    spread_step(0, 0)

    lane = lax.broadcasted_iota(jnp.int32, (1, T), 1)
    def short_rows(r):
        for j in range(3):
            z = zf[j, r]
            z1 = jnp.where(lane >= 1, pltpu.roll(z, 1, 1), 0.0)
            z2 = jnp.where(lane >= 2, pltpu.roll(z, 2, 1), 0.0)
            k = 5 + 3 * j
            sf[j, r] = pcol_r[r, k : k + 1] * z + pcol_r[r, k + 1 : k + 2] * z1 + pcol_r[r, k + 2 : k + 3] * z2
        p = sf[2, r] * sf[1, r]
        pv[r] = p
        XS[r, 0:T], XS[r, T : 2 * T] = two(p)

    chunks(C, short_rows)
    spectrum(XSh, PS)
    zero = lax.broadcasted_iota(jnp.int32, (1, T), 1) == 0
    def prod(A, B, out, conj, low=None):
        @pl.loop(0, C // ROWS)
        def _(i):
            r = pl.ds(pl.multiple_of(i * ROWS, ROWS), ROWS)
            ar, ai = A[r, 0:T], A[r, T : 2 * T]
            br, bi = B[r, 0:T], B[r, T : 2 * T]
            ii = ai * bi
            iz = jnp.where(zero, 0.0, ii)
            if conj:
                re = ar * br + iz
                im = jnp.where(zero, ii, ar * bi - ai * br)
            else:
                re = ar * br - iz
                im = jnp.where(zero, ii, ar * bi + ai * br)
            for e, x in enumerate((re, im)):
                hi, lo = two(jnp.where(zero, 0.5 * x, x))
                out[r, e * T : e * T + T] = hi
                if low is not None:
                    low[pl.ds(r.start + e * C, ROWS)] = lo

    spread_step(0, 0, True)
    spread_step(0, 1)
    relay_on(1, 4)
    relay_on(1, 5)
    spread_step(1, 0)
    prod(KS, PS, XS, False, dzf)
    inverse(yv, dzf)

    def y_rows(r):
        y = yv[r] * (1.0 / T) + pcol_r[r, 16:17] * pv[r]
        yv[r] = y
        o = (y * sf[0, r]).astype(bf)
        for b in range(MP):
            oB[b, r] = o[:, TB * b : TB * b + TB]

    chunks(C, y_rows)
    c_o = [rc(oB.at[peer[k]], oK.at[m], pdev[k]) for k in (1, 2, 3)]
    oK[m] = oB[m]
    c_ct = [rc(cotB.at[peer[k]], cotK.at[m], pdev[k]) for k in (1, 2, 3)]
    cotK[m] = cotB[m]
    spread_step(1, 0, True)
    spread_step(1, 1)
    relay_on(2, 4)
    relay_on(2, 5)
    spread_step(2, 0)
    recv(c_wo2)

    recv(c_o)
    oks = oK[...].reshape(D, TB)
    for h in range(2):
        rv[h * H : (h + 1) * H, :] = dg(WO[h].reshape(D, H), oks, 0, 0)
    tot = jnp.zeros((1, TB), f32)
    for s in range(MP):
        rr = slice(s * C, s * C + C)
        r = rv[rr] + tokF[s, m].astype(f32) + COLS[rr, 4:5]
        rv[rr] = r
        tot = tot + jnp.sum(r, axis=0, keepdims=True)
    mu = tot * (1.0 / D)
    tot = jnp.zeros((1, TB), f32)
    for s in range(MP):
        xc = rv[s * C : s * C + C] - mu
        tot = tot + jnp.sum(xc * xc, axis=0, keepdims=True)
    sc2 = lax.rsqrt(tot * (1.0 / D) + epsilon)
    stat[2:3, 0:TB] = sc2
    for s in range(MP):
        rr = slice(s * C, s * C + C)
        xh = (rv[rr] - mu) * sc2
        xh2[rr] = xh
        n2P[rr, 0:TB] = (xh * COLS[rr, 2:3] + COLS[rr, 3:4]).astype(bf)
    c_n2 = rc(n2P.at[:, pl.ds(0, TB)], n2P.at[:, pl.ds(TB, TB)], dnb[0])

    recv(c_ct)
    for s in range(MP):
        goP[s * C : s * C + C, 0:TB] = (cotK[s].astype(f32) * wt[m, 0:1, :]).astype(bf)
    c_go = rc(goP.at[:, pl.ds(0, TB)], goP.at[:, pl.ds(TB, TB)], dnb[0])

    def ffn_slot(k):
        s = slot[k]
        for blk in (1, 0):
            l = slice(blk * TB, blk * TB + TB)
            a = dg(WU[s].reshape(D, H), n2P[:, l], 0, 0) + COLS[0:H, 64 + 8 * k : 65 + 8 * k]
            cdf = 0.5 * (1.0 + lax.erf(a * (1.0 / math.sqrt(2.0))))
            gv[k, :, l] = (a * cdf).astype(bf)
            gp = cdf + a * jnp.exp(-0.5 * a * a) * (1.0 / math.sqrt(2.0 * math.pi))
            da = dg(WD[s].reshape(H, D), goP[:, l], 1, 0) * gp
            dav[k, :, l] = da.astype(bf)
            rows = pl.ds(pl.multiple_of(H * x0, H), H)
            COLS[rows, 35 + k : 36 + k] += jnp.sum(da, axis=1, keepdims=True)

    def dn2_of(blk, out):
        l = slice(blk * TB, blk * TB + TB)
        for q in range(2):
            acc = dg(WU[m, q].reshape(H, H), dav[0, :, l], 1, 0)
            for k in range(1, MP):
                acc = acc + dg(WU[slot[k], q].reshape(H, H), dav[k, :, l], 1, 0)
            out[q * H : (q + 1) * H] = acc.astype(out.dtype)

    def br_of(blk, out):
        l = slice(blk * TB, blk * TB + TB)
        for q in range(0, D, H):
            acc = dg(WD[m, :, :, :, q : q + H].reshape(H, H), gv[0, :, l], 0, 0)
            for k in range(1, MP):
                acc = acc + dg(WD[slot[k], :, :, :, q : q + H].reshape(H, H), gv[k, :, l], 0, 0)
            out[q : q + H] = acc.astype(out.dtype)

    def ffn_grads(k):
        for h in range(2):
            gu = dg(n2P[h * H : (h + 1) * H], dav[k], 1, 1).astype(bf)
            gd = dg(gv[k, h * H // 2 : (h + 1) * H // 2], goP[...], 1, 1).astype(bf)
            for i in range(2):
                GU[k // 2, h, i, k % 2] = gu[i * QU : (i + 1) * QU, :]
                GD[k // 2, h, i, k % 2] = gd[i * QD : (i + 1) * QD, :]

    class Reduce:
        def __init__(self, order, G, R, X, FIN):
            self.x = [bits[o] for o in order]
            self.nb = [dnb[o] for o in order]
            self.n = len(order)
            self.G, self.R, self.X, self.FIN = G, R, X, FIN
            self.step = 0
            self.c = None

        def at(self, ref, k, flip=False):
            idx = list(self.x[:k])
            if flip:
                idx[-1] = 1 - idx[-1]
            return ref.at[tuple(idx)]

        def send(self):
            self.c = rc(self.at(self.G, self.step + 1, True), self.R[self.step], self.nb[self.step])

        def add(self):
            self.c.wait_recv()

            def one(g, r):
                if len(g.shape) > 2:
                    for a in range(g.shape[0]):
                        one(g.at[a], r.at[a])
                    return
                n = g.shape[0]

                def rows(q):
                    g[q] = (g[q].astype(f32) + r[q].astype(f32)).astype(bf)

                chunks(n, rows, 48)

            one(self.at(self.G, self.step + 1), self.R[self.step])
            self.step += 1

        def piece(self):
            return self.at(self.G, self.n)

        def extra(self):
            for e, b in enumerate(range(3, nbits)):
                bufs = self.X(e)
                parts = [self.piece()] if len(bufs) == 1 else [self.piece().at[pl.ds(2 * i, 2)] for i in range(2)]
                cs = [rc(p, x, dnb[b]) for p, x in zip(parts, bufs)]
                sent(cs)
                recv(cs)
                for p, x in zip(parts, bufs):
                    p[...] = (p[...].astype(f32) + x[...].astype(f32)).astype(bf)

        def gather(self):
            k = 2 * self.n - self.step
            ref = self.at(self.FIN, k)
            self.c = rc(ref, ref, self.nb[k - 1])
            self.step += 1

        def got(self):
            self.c.wait_recv()

    spare = lambda W, R, g: lambda e: [W.at[2 + e, g] if e < 2 else R]
    rU = [Reduce((1, 2), GU.at[g], [RU0.at[g], RU1.at[g]], spare(WU, RU1.at[g], g), FU.at[x0]) for g in range(2)]
    rD = [Reduce((2, 1), GD.at[g], [RD0.at[g], RD1.at[g]], spare(WD, RD1.at[g], g), FD.at[x0]) for g in range(2)]
    recv([c_go, c_n2])
    ffn_slot(0)
    spread_step(2, 0, True)
    spread_step(2, 1)
    spread_step(0, 1, True)
    ffn_slot(1)
    ffn_grads(0)
    ffn_grads(1)
    rU[0].send()
    rD[0].send()
    spread_step(1, 1, True)
    ffn_slot(2)
    spread_step(2, 1, True)
    ffn_slot(3)
    dn2_of(1, dnS)
    c_dn = rc(dnS, dnR, dnb[0])
    dn2_of(0, dnO)

    recv([c_dn])
    sent(c_ct)
    t1 = jnp.zeros((1, TB), f32)
    t2 = jnp.zeros((1, TB), f32)
    for s in range(MP):
        rr = slice(s * C, s * C + C)
        dn2 = dnO[rr] + dnR[rr].astype(f32)
        dnO[rr] = dn2
        xh = xh2[rr]
        dx = dn2 * xh
        COLS[rr, 33:34] = jnp.sum(dx, axis=1, keepdims=True)
        COLS[rr, 34:35] = jnp.sum(dn2, axis=1, keepdims=True)
        t1 = t1 + jnp.sum(dn2 * COLS[rr, 2:3], axis=0, keepdims=True)
        t2 = t2 + jnp.sum(dx * COLS[rr, 2:3], axis=0, keepdims=True)
    m1, m2 = t1 * (1.0 / D), t2 * (1.0 / D)
    for s in range(MP):
        rr = slice(s * C, s * C + C)
        dr = cotK[s].astype(f32) * wt[m, 0:1, :] + stat[2:3, 0:TB] * (dnO[rr] * COLS[rr, 2:3] - m1 - xh2[rr] * m2)
        COLS[rr, 32:33] = jnp.sum(dr, axis=1, keepdims=True)
        drS[s] = dr.astype(bf)
    drl = drS[...].reshape(D, TB)
    do = dg(WO[0].reshape(D, H), drl[0:H, :], 1, 0) + dg(WO[1].reshape(D, H), drl[H:D, :], 1, 0)
    doS[...] = do.astype(bf).reshape(MP, C, TB)
    c_do = [rc(doS.at[peer[k]], doB.at[m], pdev[k]) for k in (1, 2, 3)]
    doB[m] = doS[m]
    c_dr = [rc(drS.at[peer[k]], drB.at[m], pdev[k]) for k in (1, 2, 3)]
    drB[m] = drS[m]

    ffn_grads(2)
    ffn_grads(3)
    rU[1].send()
    rD[1].send()

    oks = oK[...].reshape(D, TB)
    rO = Reduce(ordO, GO, [RO0, RO1, RO2], lambda e: [WO.at[0, e]], FO)
    for s in range(MP):
        gw = dg(oK[s], drl, 1, 1).astype(bf)
        for i in range(8):
            GO[i // 4, (i // 2) % 2, i % 2, s * WR : (s + 1) * WR, :] = gw[
                WR * (i % 4) : WR * (i % 4) + WR, H * (i // 4) : H * (i // 4) + H
            ]
    rO.send()

    br_of(1, brS)
    c_br = rc(brS, brR, dnb[0])
    br_of(0, brO)

    @pl.when(m < MP - 1)
    def _():
        pl.semaphore_signal(gfree, inc=1, device_id=right, device_id_type=MESH)

    @pl.when(m > 0)
    def _():
        pl.semaphore_signal(gfree, inc=1, device_id=left, device_id_type=MESH)

    recv([c_br])
    sent(c_o)
    for s in range(MP):
        rr = slice(s * C, s * C + C)
        outS[s] = (rv[rr] + brO[rr] + brR[rr].astype(f32) + COLS[rr, 5:6]).astype(bf)
    c_out = [rc(outS.at[peer[k]], outB.at[m], pdev[k]) for k in (1, 2, 3)]
    outB[m] = outS[m]
    rU[0].add()
    rU[0].send()
    rD[0].add()
    rD[0].send()
    rO.add()
    rO.send()

    recv(c_do)
    for b in range(MP):
        l = slice(TB * b, TB * b + TB)
        dO = doB[b].astype(f32)
        dyb = dO * sf[0, :, l]
        dsv[0, :, l] = dyb
        XS[:, l], XS[:, T + TB * b : T + TB * b + TB] = two(dyb)
        yv[:, l] = dO * yv[:, l]
    spectrum(XSh, dks)
    prod(KS, dks, XS, True)
    inverse(dsv.at[1])

    def back_rows(r):
        dy = dsv[0, r]
        SAc[r, 16:17] = jnp.sum(dy * pv[r], axis=1, keepdims=True)
        dgt = dsv[1, r] * (1.0 / T) + pcol_r[r, 16:17] * dy
        for j in range(3):
            ds = yv[r] if j == 0 else dgt * sf[3 - j, r]
            d1 = jnp.where(lane < T - 1, pltpu.roll(ds, T - 1, 1), 0.0)
            d2 = jnp.where(lane < T - 2, pltpu.roll(ds, T - 2, 1), 0.0)
            k = 5 + 3 * j
            dz = pcol_r[r, k : k + 1] * ds + pcol_r[r, k + 1 : k + 2] * d1 + pcol_r[r, k + 2 : k + 3] * d2
            dzf[pl.ds(r.start + j * C, ROWS)] = dz.astype(bf)
            SAc[r, 2 + j : 3 + j] = jnp.sum(dz, axis=1, keepdims=True)
            z = zf[j, r]
            SAc[r, k : k + 1] = jnp.sum(ds * z, axis=1, keepdims=True)
            SAc[r, k + 1 : k + 2] = jnp.sum(d1 * z, axis=1, keepdims=True)
            SAc[r, k + 2 : k + 3] = jnp.sum(d2 * z, axis=1, keepdims=True)

    chunks(C, back_rows)

    for step in range(3):
        for b in range(NC):
            sent_right = (m < MP - 1) if step == 0 else jnp.logical_and(m - step >= 0, m < MP - 1)
            sent_left = (m > 0) if step == 0 else jnp.logical_and(m + step < MP, m > 0)

            @pl.when(sent_right)
            def _():
                relay(0, step, b, m - step, right).wait_send()

            @pl.when(sent_left)
            def _():
                relay(1, step, b, m + step, left).wait_send()

    for step in range(3):
        for stage in range(2):
            spread_step(step, stage, "send")

    dn1S = tokF

    def dn1R(slot, b):
        return (gv if slot < 4 else dav).at[slot % 4 // 2 * 2 + b // 2, pl.ds(b % 2 * C, C), pl.ds(slot % 2 * TB, TB)]

    def rs_copy(way, s, b, dev, last=False):
        i = (way * MP + s) * MP + b
        return pltpu.make_async_remote_copy(
            src_ref=dn1S.at[s, b], dst_ref=dn1R(MP if last and way == 1 else s, b),
            send_sem=ss_rs.at[i], recv_sem=rs_rs.at[i], device_id=dev, device_id_type=MESH,
        )

    inner = jnp.logical_and(m > 0, m < MP - 1)

    @pl.when(inner)
    def _():
        pl.semaphore_wait(gfree, 2)

    @pl.when(jnp.logical_not(inner))
    def _():
        pl.semaphore_wait(gfree, 1)

    for b in range(MP):
        l = slice(TB * b, TB * b + TB)
        part = dg(winv[0], dzf[0:C, l], 0, 0)
        for j in (1, 2):
            part = part + dg(winv[j], dzf[j * C : (j + 1) * C, l], 0, 0)
        for s in (0, 3, 1, 2):
            own = part[s * C : (s + 1) * C]

            @pl.when(m == s)
            def _():
                dsv[0, :, l] = own

            @pl.when(m != s)
            def _():
                dn1S[s, b] = own.astype(bf)

            if s < MP - 1:
                @pl.when(m == MP - 1)
                def _():
                    rs_copy(1, s, b, left, s == MP - 2).start()
            if s > 0:
                @pl.when(m == 0)
                def _():
                    rs_copy(0, s, b, right).start()

    def rs_forward(b):
        for way, s in ((1, 0), (0, 3), (1, 1), (0, 2)):
            for mm in range(1, MP - 1):
                if (way == 1 and mm > s) or (way == 0 and mm < s):
                    last = mm - 1 == s if way == 1 else mm + 1 == s

                    @pl.when(m == mm)
                    def _():
                        rs_copy(way, s, b, left if way == 1 else right).wait_recv()
                        dn1S[s, b] = (dn1S[s, b].astype(f32) + dn1R(s, b)[...].astype(f32)).astype(bf)
                        rs_copy(way, s, b, left if way == 1 else right, last).start()

    rI = Reduce(ordO, GI, [RI0, RI1, RI2], lambda e: [XGI.at[e]], FI)
    PI = 3 * C // 4
    for h in range(2):
        gi = dg(dzf[h * 2 * PI : (h + 1) * 2 * PI, :], n1F[...], 1, 1).astype(bf)
        for i in range(2):
            for e in range(2):
                GI[e, h, i] = gi[i * PI : (i + 1) * PI, e * H : (e + 1) * H]
    rI.send()
    rs_forward(0)
    rU[1].add()
    rU[1].send()
    rD[1].add()
    rD[1].send()
    rs_forward(1)
    rU[0].add()
    rD[0].add()
    for e, b in enumerate(range(3, nbits)):
        pl.semaphore_signal(credit.at[e], inc=1, device_id=dnb[b], device_id_type=MESH)
    for e in range(nbits - 3):
        pl.semaphore_wait(credit.at[e], 1)
    rU[0].extra()
    rD[0].extra()
    c_z = {}

    def cross(k):
        for i, (r, Rz) in enumerate(((rU, RUz), (rD, RDz))):
            c_z[k, i] = rc(r[k // 2].piece().at[k % 2], Rz.at[k - 1], pdev[k])


    prod(PS, dks, XS, True, dzf)
    inverse(dsv.at[1], dzf)
    share = pen_coef / (D * dp_size)

    def filter_rows(r):
        kern = kv[r]
        k2 = kern * kern
        tail = jnp.sum(jnp.where(lane >= T // 2, k2, 0.0), axis=1, keepdims=True) * (2.0 / T)
        whole = jnp.sum(k2, axis=1, keepdims=True) * (1.0 / T) + 1e-06
        iw = 1.0 / whole
        ratio = tail * iw
        coef = jnp.where(lane >= T // 2, iw * (4.0 / T), 0.0) - ratio * iw * (2.0 / T)
        dkt = dsv[1, r] * (1.0 / T) + share * coef * kern
        SAc[r, 15:16] = -jnp.sum(dkt * kern * tramp, axis=1, keepdims=True)
        SAc[r, 18:19] = ratio
        draw = dkt * jnp.exp(-pcol_r[r, 15:16] * tramp)
        SAc[r, 14:15] = jnp.sum(draw, axis=1, keepdims=True)
        dsv[1, r] = draw

    chunks(C, filter_rows)
    rI.add()
    rI.send()
    rO.add()
    rO.send()
    rs_forward(2)
    h2 = h2s[...]
    h1 = h1s[...]
    w2 = u2s[...]
    w1 = u1s[...]
    draw = dsv[1]
    SM1[32 : 32 + FILT, :] = dg(h2, draw, 1, 1, precision=HI)
    dh2 = dg(f3_r[...], draw, 1, 0, precision=HI)
    e2 = dh2 * jnp.cos(q1s * w2)
    dw2 = e2 * q1s
    SM3[40 : 40 + FILT, :] = dg(h1, dw2, 1, 1, precision=HI)
    dh1 = dg(f2_r[...], dw2, 1, 0, precision=HI)
    e1 = dh1 * jnp.cos(q0 * w1)
    dw1 = e1 * q0
    SM3[0:40, :] = dg(emb[...], dw1, 1, 1, precision=HI)[0:40]
    fz[...] = jnp.zeros_like(fz)
    cols = (dw1, dw2, e1 * w1, e2 * w2)
    for i, col in enumerate(cols):
        fz[0:FILT, i : i + 1] = jnp.sum(col, axis=1, keepdims=True)
    fz[0:1, 4:5] = jnp.sum(SAc[:, 18:19], axis=0, keepdims=True) * (1.0 / (D * dp_size))
    SM3[40 + FILT : 48 + FILT, :] = fz[0:FILT, :].T[0:8, :]
    SM1[0:32, :] = SAc[...].T[0:32, :]
    SM2[...] = COLS[...].T[32:40, :]

    def hop(b, cur, got):
        cs = [rc(x, y.at[b], dnb[b]) for x, y in zip(cur, got)]

        def finish():
            recv(cs)
            for x, y in zip(cur, got):
                y[b] = y[b] + x[...]
            return [y.at[b] for y in got]

        return finish

    sm_got = (SM1r, SM2r, SM3r)
    hop_sm = hop(0, [SM1, SM2, SM3], sm_got)
    rU[1].add()
    rD[1].add()
    for e, b in enumerate(range(3, nbits)):
        pl.semaphore_signal(credit.at[e], inc=1, device_id=dnb[b], device_id_type=MESH)
    for e in range(nbits - 3):
        pl.semaphore_wait(credit.at[e], 1)
    rU[1].extra()
    rD[1].extra()
    for mm, way in ((0, 0), (MP - 1, 1)):
        @pl.when(m == mm)
        def _():
            for b in range(MP):
                for s in range(MP):
                    if s != mm:
                        rs_copy(way, s, b, right if way == 0 else left).wait_send()

    for k in (1, 2, 3):
        cross(k)

    rO.add()
    rO.extra()
    c_zo = [rc(rO.piece().at[pl.ds(WR * peer[k], WR)], RO3.at[k - 1], pdev[k]) for k in (1, 2, 3)]
    recv(c_out)
    c_outh = lc(outB, outb_o)
    cur = hop_sm()
    hop_sm = hop(1, cur, sm_got)
    early = list(pending)
    rs_forward(3)
    cur = hop_sm()
    hop_sm = hop(2, cur, sm_got)
    rI.add()
    rI.send()

    rI.add()
    rI.extra()
    FI[x0, x1, x2] = rI.piece()[...]
    rI.gather()

    sent([c for c in early if any(c is p for p in pending)])
    recv(c_zo + list(c_z.values()))
    for r, Rz in ((rU[0], RUz), (rD[0], RDz)):
        own = r.piece()[0].astype(f32)
        for k in range(3):
            own = own + Rz[k].astype(f32)
        r.FIN[r.x[0], r.x[1]] = own.astype(bf)
        r.gather()
    own = rO.piece()[pl.ds(WR * m, WR), :].astype(f32)
    for k in range(3):
        own = own + RO3[k].astype(f32)
    FO[x0, x1, x2] = own.astype(bf)
    rO.gather()

    for mm in range(MP):
        @pl.when(m == mm)
        def _():
            for b in range(MP):
                l = slice(TB * b, TB * b + TB)
                if mm < MP - 1:
                    rs_copy(1, mm, b, left, True).wait_recv()
                    dsv[0, :, l] += dn1R(MP, b)[...].astype(f32)
                if mm > 0:
                    rs_copy(0, mm, b, right).wait_recv()
                    dsv[0, :, l] += dn1R(mm, b)[...].astype(f32)

    dn1 = dsv[0]
    q1 = dn1 * pcol_r[:, 0:1]
    for b in range(MP):
        l = slice(TB * b, TB * b + TB)
        xhb = (tokF[m, b].astype(f32) - stat[0:1, l]) * stat[1:2, l]
        yv[:, l] = xhb
    xh1 = yv[...]
    stS[0:1, :] = jnp.sum(q1, axis=0, keepdims=True)
    stS[1:2, :] = jnp.sum(q1 * xh1, axis=0, keepdims=True)
    c_st = [rc(stS, stR.at[k - 1], pdev[k]) for k in (1, 2, 3)]
    SM4[...] = jnp.zeros_like(SM4)
    SAc[:, 0:1] = jnp.sum(dn1 * xh1, axis=1, keepdims=True)
    SAc[:, 1:2] = jnp.sum(dn1, axis=1, keepdims=True)
    SM4[...] = SAc[...].T[0:8, :]
    h4 = hop(0, [SM4], [SM4r])
    for b in range(3, nbits):
        cur = hop_sm()
        hop_sm = hop(b, cur, sm_got)
    SM1, SM2, SM3 = hop_sm()
    c_s1 = [rc(SM3, SMz3.at[k - 1], pdev[k]) for k in (1, 2, 3)]
    c_s2 = [rc(SM2, SMz2.at[k - 1], pdev[k]) for k in (1, 2, 3)]
    outs = [lc(SM1, sm1_o)]
    rI.got()
    rI.gather()
    cur4 = h4()
    h4 = hop(1, cur4, [SM4r])
    cur4 = h4()
    h4 = hop(2, cur4, [SM4r])
    rU[0].got()
    rU[0].gather()
    rD[0].got()
    rD[0].gather()
    rI.got()
    rI.gather()
    rO.got()
    rO.gather()
    recv(c_st)
    tot = stS[0:2, :]
    for k in range(3):
        tot = tot + stR[k, 0:2, :]
    recv(c_dr)
    for b in range(MP):
        l = slice(TB * b, TB * b + TB)
        back = stat[1:2, l] * (q1[:, l] - tot[0:1, l] * (1.0 / D) - xh1[:, l] * (tot[1:2, l] * (1.0 / D)))
        dsv[1, :, l] = drB[b].astype(f32) + back
    c_dtok = lc(dsv.at[1], dtok_o)
    for b in range(3, nbits):
        cur4 = h4()
        h4 = hop(b, cur4, [SM4r])
    recv(c_s1)
    recv(c_s2)
    a3 = SM3[...]
    for k in range(3):
        a3 = a3 + SMz3[k]
    SMz3[0] = a3
    outs.append(lc(SMz3.at[0], sm3_o))
    a2 = SM2[...]
    for k in range(3):
        a2 = a2 + SMz2[k]
    dbu = SM2[3:4, :]
    for k in range(3):
        dbu = dbu + SMz2[k, 4 + k : 5 + k, :]
    SMz2[0] = jnp.broadcast_to(dbu, (8, D))
    outs.append(lc(SMz2.at[0], sm2_o))
    for mm in range(MP):
        @pl.when(m == mm)
        def _():
            prow[2:5, :] = a2[0:3, mm * C : (mm + 1) * C]
    rU[0].got()
    rD[0].got()
    c_fu = rc(FU.at[x0], FU.at[x0], dnb[0])
    c_fd = rc(FD.at[x0], FD.at[x0], dnb[0])
    outs += [lc(FU.at[x0], gup_o.at[x0]), lc(FD.at[x0], gdn_o.at[x0])]
    rO.got()
    rO.gather()
    rI.got()
    outs.append(lc(FI, gin_o))
    cur4 = h4()
    prow[0:2, :] = cur4[0][0:2, :]
    outs.append(lc(prow.at[pl.ds(0, 8)], sm4_o))
    recv([c_fu, c_fd])
    outs += [lc(FU.at[1 - x0], gup_o.at[1 - x0]), lc(FD.at[1 - x0], gdn_o.at[1 - x0])]
    rO.got()
    outs.append(lc(FO, gwo_o))
    for c in outs + [c_dtok, c_outh]:
        c.wait()

    for c in pending:
        c.wait_send()
    for s in range(MP):
        if s < MP - 1:
            @pl.when(jnp.logical_and(m > s, m < MP - 1))
            def _():
                for b in range(MP):
                    rs_copy(1, s, b, left).wait_send()
        if s > 0:
            @pl.when(jnp.logical_and(m < s, m > 0))
            def _():
                for b in range(MP):
                    rs_copy(0, s, b, right).wait_send()


def finish_kernel(
    outb, dtok, gup, gdn, gwo, gin, sm1, sm2, sm3, sm4,
    out_o, dtok_o, dg1, ds1, dwin_o, dbin, dtaps, df1, dc1, df2, dc2, dsq, df3, dc3, ddec, dcb,
    dwout_o, dbo, dg2, ds2, dwup_o, dbu, dwdn_o, dbd, pen,
    vout, vdt, vup, vdn, vwo, vin, fout, fup, fdn, fwo, fin, isem, osem,
):
    MPN, C, TB = vout.shape
    ins = [(outb, vout), (dtok, vdt), (gup, vup), (gdn, vdn), (gwo, vwo), (gin, vin)]
    cin = [pltpu.make_async_copy(a, b, isem.at[i]) for i, (a, b) in enumerate(ins)]
    for i in (2, 3, 0, 1, 5, 4):
        cin[i].start()
    cout = []

    def put(src, dst):
        c = pltpu.make_async_copy(src, dst, osem.at[len(cout)])
        c.start()
        cout.append(c)

    PR, D = vdn.shape[3:]
    H = D // 2
    cin[2].wait()
    for e in range(2):
        fup[:, e * H : (e + 1) * H] = vup[e].reshape(D, H).astype(f32)
    put(fup, dwup_o)
    cin[3].wait()
    for e in range(2):
        fdn[e * H : (e + 1) * H, :] = vdn[e].reshape(H, D).astype(f32)
        put(fdn.at[pl.ds(e * H, H)], dwdn_o.at[pl.ds(e * H, H)])
    cin[0].wait()
    for b in range(MPN):
        fout[:, TB * b : TB * b + TB] = vout[b].astype(f32)
    put(fout, out_o)
    cin[1].wait()
    put(vdt, dtok_o)
    cin[5].wait()
    for e in range(2):
        fin[:, e * H : (e + 1) * H] = vin[e].reshape(3 * C, H).astype(f32)
    put(fin, dwin_o)
    cin[4].wait()
    for e in range(2):
        fwo[:, e * H : (e + 1) * H] = vwo[e].reshape(C, H).astype(f32)
    put(fwo, dwout_o)
    for o, r in ((dg1, sm4[0:1]), (ds1, sm4[1:2]), (dbo, sm4[2:3]), (dg2, sm4[3:4]), (ds2, sm4[4:5]),
                 (dc3, sm1[14:15]), (ddec, sm1[15:16]), (dcb, sm1[16:17]), (dbd, sm1[17:18])):
        o[...] = r.reshape(C)
    dbu[...] = sm2[0:1].reshape(D)
    dbin[...] = sm1[2:5]
    for j in range(3):
        dtaps[j] = sm1[5 + 3 * j : 8 + 3 * j]
    df3[...] = sm1[32 : 32 + FILT]
    df1[...] = sm3[0:EMB]
    df2[...] = sm3[40 : 40 + FILT]
    dc1[...] = sm3[40 + FILT : 41 + FILT].reshape(FILT)
    dc2[...] = sm3[41 + FILT : 42 + FILT].reshape(FILT)
    dsq[...] = sm3[42 + FILT : 44 + FILT]
    pen[...] = sm3[44 + FILT : 45 + FILT, 0:1]
    for c in cout:
        c.wait()


def build(dp_size):
    nbits = int(math.log2(dp_size))

    def per_device(
        tokens, cotangent, seg_ids, row_lengths, group_tags, group_weights, gain_one, shift_one,
        w_in, b_in, taps, f_one, c_one, f_two, c_two, sine_freq, f_three, c_three, decay, conv_bias,
        w_out, b_out, gain_two, shift_two, w_up, b_up, w_down, b_down,
    ):
        T, C = tokens.shape
        D = C * MP
        TB = T // MP
        fwd, emb = tables(T)
        V = pltpu.VMEM
        PR, WR, H, PI = D // 8, C // 4, D // 2, 3 * C // 4
        ne = max(nbits - 3, 1)
        scratch = dict(
            tokF=V((MP, MP, C, TB), bf), cotB=V((MP, C, TB), bf),
            cotK=V((MP, C, TB), bf), n1F=V((D, T), bf), winv=V((3, C, D), bf), F=V((T, 2 * T), bf),
            emb=V((128, T), f32), zf=V((3, C, T), f32), sf=V((3, C, T), f32),
            yv=V((C, T), f32), pv=V((C, T), f32), kv=V((C, T), f32), KS=V((C, 2 * T), f32),
            PS=V((C, 2 * T), f32), XS=V((C, 2 * T), bf),
            oB=V((MP, C, TB), bf), oK=V((MP, C, TB), bf), WO=V((2, MP, C, H), bf), WU=V((MP, 2, 2, D // 4, H), bf), WD=V((MP, 2, 2, PR, D), bf),
            rv=V((D, TB), f32), xh2=V((D, TB), f32), n2P=V((D, 2 * TB), bf), goP=V((D, 2 * TB), bf),
            gv=V((MP, H, 2 * TB), bf), dav=V((MP, H, 2 * TB), bf), wt=V((MP, 8, TB), f32), stat=V((8, T), f32),
            PG=V((MP, 8, C), f32), COLS=V((D, 128), f32),
            brS=V((D, TB), bf), brR=V((D, TB), bf), dnS=V((D, TB), bf), dnR=V((D, TB), bf),
            outB=V((MP, C, TB), bf), drB=V((MP, C, TB), bf),
            doS=V((MP, C, TB), bf), doB=V((MP, C, TB), bf), dnO=V((D, TB), f32), brO=V((D, TB), f32),
            GU=V((2, 2, 2, 2, D // 4, H), bf), RU0=V((2, 2, 2, D // 4, H), bf), RU1=V((2, 2, D // 4, H), bf), RUz=V((3, D // 4, H), bf),
            GD=V((2, 2, 2, 2, PR, D), bf), RD0=V((2, 2, 2, PR, D), bf), RD1=V((2, 2, PR, D), bf), RDz=V((3, PR, D), bf),
            GO=V((2, 2, 2, C, H), bf), RO0=V((2, 2, C, H), bf), RO1=V((2, C, H), bf), RO2=V((C, H), bf),
            RO3=V((3, WR, H), bf), FO=V((2, 2, 2, WR, H), bf),
            GI=V((2, 2, 2, PI, H), bf), RI0=V((2, 2, PI, H), bf), RI1=V((2, PI, H), bf), RI2=V((PI, H), bf),
            FI=V((2, 2, 2, PI, H), bf),
            dzf=V((3 * C, T), bf),
            stS=V((8, T), f32), stR=V((3, 8, T), f32), SAc=V((C, 128), f32),
            SM1=V((96, C), f32), SM1r=V((nbits, 96, C), f32), SM3=V((48 + FILT, FILT), f32), SM3r=V((nbits, 48 + FILT, FILT), f32), SM2=V((8, D), f32), SM2r=V((nbits, 8, D), f32),
            SMz3=V((3, 48 + FILT, FILT), f32), SMz2=V((3, 8, D), f32), SM4=V((8, C), f32), SM4r=V((nbits, 8, C), f32),
            XGI=V((ne, PI, H) if nbits > 3 else (1, 16, 128), bf),
            h1s=V((FILT, T), f32), h2s=V((FILT, T), f32), u1s=V((FILT, T), f32), u2s=V((FILT, T), f32),
            dks=V((C, 2 * T), f32), dsv=V((2, C, T), f32), prow=V((32, C), f32), pcol_r=V((C, 32), f32), bup=V((MP, 8, H), f32), fz=V((128, FILT), f32), frow=V((8, FILT), f32),
            gfree=pltpu.SemaphoreType.REGULAR, credit=pltpu.SemaphoreType.REGULAR((ne,)), ssem=pltpu.SemaphoreType.DMA((NSEM,)), rsem=pltpu.SemaphoreType.DMA((NSEM,)),
            lsem=pltpu.SemaphoreType.DMA((40,)), ss_tok=pltpu.SemaphoreType.DMA((36,)), rs_tok=pltpu.SemaphoreType.DMA((36,)),
            ss_rs=pltpu.SemaphoreType.DMA((32,)), rs_rs=pltpu.SemaphoreType.DMA((32,)), ss_sp=pltpu.SemaphoreType.DMA((24,)), rs_sp=pltpu.SemaphoreType.DMA((24,)),
        )
        anyspec = pl.BlockSpec(memory_space=pl.ANY)
        vm = pl.BlockSpec(memory_space=pltpu.VMEM)
        sm = pl.BlockSpec(memory_space=pltpu.SMEM)
        S = jax.ShapeDtypeStruct
        outs = pl.pallas_call(
            functools.partial(main_kernel, nbits, dp_size, (T, C, D)),
            out_shape=[
                S((MP, C, TB), bf), S((C, T), f32), S((2, 2, 2, D // 4, H), bf), S((2, 2, 2, PR, D), bf),
                S((2, 2, 2, WR, H), bf), S((2, 2, 2, PI, H), bf), S((96, C), f32), S((8, D), f32),
                S((48 + FILT, FILT), f32), S((8, C), f32),
            ],
            in_specs=[anyspec] * 8 + [vm, sm, sm, sm] + [vm] * 18,
            out_specs=[anyspec] * 10,
            scratch_shapes=list(scratch.values()),
            compiler_params=pltpu.CompilerParams(
                collective_id=0, has_side_effects=True, vmem_limit_bytes=63 * 2**20
            ),
            name="hyena_block",
        )(
            tokens.T, cotangent.T, jnp.transpose(w_in, (0, 2, 1)), w_out, w_up, w_down, jnp.asarray(fwd), jnp.asarray(emb),
            seg_ids, row_lengths, group_tags, group_weights, gain_one, shift_one, b_in, taps, f_one, c_one,
            f_two, c_two, sine_freq, f_three, c_three, decay, conv_bias, b_out, gain_two, shift_two, b_up, b_down,
        )
        v1, vF, v2 = S((C,), f32), S((FILT,), f32), S((2, FILT), f32)
        res = pl.pallas_call(
            finish_kernel,
            out_shape=[
                S((C, T), f32), S((C, T), f32), v1, v1, S((3 * C, D), f32), S((3, C), f32), S((3, 3, C), f32),
                S((EMB, FILT), f32), vF, S((FILT, FILT), f32), vF, v2, S((FILT, C), f32), v1, v1, v1,
                S((C, D), f32), v1, v1, v1, S((D, D), f32), S((D,), f32), S((D, D), f32), v1, S((1, 1), f32),
            ],
            in_specs=[anyspec] * 6 + [vm] * 4,
            out_specs=[anyspec if i in (0, 1, 4, 16, 20, 22) else vm for i in range(25)],
            scratch_shapes=[
                V((MP, C, TB), bf), V((C, T), f32), V((2, 2, 2, D // 4, H), bf), V((2, 2, 2, PR, D), bf), V((2, 2, 2, WR, H), bf),
                V((2, 2, 2, PI, H), bf), V((C, T), f32), V((D, D), f32), V((D, D), f32), V((C, D), f32), V((3 * C, D), f32),
                pltpu.SemaphoreType.DMA((6,)), pltpu.SemaphoreType.DMA((8,)),
            ],
            compiler_params=pltpu.CompilerParams(vmem_limit_bytes=63 * 2**20),
            name="hyena_finish",
        )(*outs)
        res = list(res)
        res[0], res[1] = res[0].T, res[1].T
        res[4] = jnp.transpose(res[4].reshape(3, C, D), (0, 2, 1))
        res[24] = res[24].reshape(())
        return tuple(res)

    return per_device


def solution(mesh):
    placed = (
        P("dp", "mp"), P("dp", "mp"), P("dp", None), P("dp"), P("dp", None), P(), P("mp"), P("mp"),
        P(None, None, "mp"), P(None, "mp"), P(None, None, "mp"), P(), P(), P(), P(), P(),
        P(None, "mp"), P("mp"), P("mp"), P("mp"), P("mp", None), P("mp"), P("mp"), P("mp"),
        P(None, "mp"), P("mp"), P("mp", None), P("mp"),
    )
    out_specs = (
        P("dp", "mp"), P("dp", "mp"), P("mp"), P("mp"), P(None, None, "mp"), P(None, "mp"),
        P(None, None, "mp"), P(), P(), P(), P(), P(), P(None, "mp"), P("mp"), P("mp"), P("mp"),
        P("mp", None), P("mp"), P("mp"), P("mp"), P(None, "mp"), P("mp"), P("mp", None), P("mp"), P(),
    )
    return jax.shard_map(
        build(mesh.shape["dp"]), mesh=mesh, in_specs=placed, out_specs=out_specs, check_vma=False
    )
```
